32 devices in a mesh: grp: 2 (over y), row: 4 (over z), col: 4 (over x, core).
Axes of the slice: x: 2, y: 2, z: 4, core: 2. Of those that a mesh axis runs over, the one named last changes fastest.
Arguments:
- mask_param: float32 [2048, 1024], P(('grp', 'row'), 'col'), parts along dimension 0, may hold values from -6 to 6
- target: bfloat16 [2048, 1024], P(('grp', 'row'), 'col'), parts along dimension 0, may hold values from 0 to 1
- kernel_modes: float32 [12, 64, 128], replicated, may hold values from -24 to 24, as said below
- kernel_weight: float32 [12], replicated, may hold values from 0.02 to 0.2
Outputs:
- healed_param: float32 [2048, 1024], P(('grp', 'row'), 'col'), parts along dimension 0
The draws below stay inside these ranges and needn't reach their ends.
There are 2 independent parts, one for each index of `grp`. The reference program is written for one: setup_inputs(seed, part) draws one part's arguments, and reference() takes and returns one part's arrays. A program takes and returns all parts, laid end to end along the dimension named above; an argument that names none is the same for every part. Nothing has to cross between parts.
Inputs may be any that keep to these rules, and one draw needn't show every extreme that they name: `kernel_modes`: the response of every kernel at the zero-frequency mode (row 32, columns 32 and 96) is zero.
All inputs are finite; a program needn't handle non-finite values.
Results may differ from the reference program's by a relative error of at most 0.0095.
Values may be sent and summed in bfloat16 or wider, within the bound.
A program may use at most 64 MiB of HBM per device.

```python
import math
import jax
import jax.numpy as jnp
from jax import lax

TILE = 256
MARGIN = 64
MODES = 64
KERN = 12
HALF = 128
WIN = 384
ROWS = 1024
COLS = 1024
N_ROW = 4
N_COL = 4


def draw_kernel_modes(key, part):
    shape = (KERN, MODES, 2 * MODES)
    base = jnp.clip(jax.random.normal(key, shape, jnp.float32), -6.0, 6.0)
    level = 0.6 * WIN / MODES
    rows_idx = jnp.arange(MODES, dtype=jnp.int32)[:, None]
    cols_idx = jnp.arange(2 * MODES, dtype=jnp.int32)[None, :]
    centre = (rows_idx == MODES // 2) & (jnp.mod(cols_idx, MODES) == MODES // 2)
    return jnp.where(centre[None], 0.0, level * base).astype(jnp.float32)


def level_of(rng, extent, cuts, low, largest):
    def one(axis_at, shards_of):
        heights = jax.random.uniform(jax.random.fold_in(jax.random.fold_in(rng, 6), axis_at), (shards_of,), jnp.float32, low / len(cuts), largest / len(cuts))
        return jnp.repeat(jnp.exp(heights), extent[axis_at] // shards_of).reshape((-1,) + (1,) * (len(extent) - axis_at - 1))

    loudness = one(*cuts[0])
    for cut in cuts[1:]:
        loudness = loudness * one(*cut)
    return loudness


def bell_draw(own_key, shape, deviation, most, cuts=(), held_as=jnp.bfloat16):
    drawn = deviation * jax.random.normal(own_key, shape, jnp.float32)
    if cuts:
        drawn = drawn * level_of(own_key, shape, cuts, -0.22, 0.18)
    return jnp.clip(drawn, -most, most).astype(held_as)


def setup_inputs(seed: int = 0, part: int = 0) -> dict:
    key_list = jax.random.split(jax.random.key(seed), 5)
    part_keys = jax.random.split(jax.random.fold_in(key_list[4], part), 5)
    mask_param = bell_draw(part_keys[0], (ROWS, COLS), 1.5, 6.0, ((0, 4), (1, 4)), jnp.float32)
    target = jnp.clip(1.0 * jax.random.uniform(part_keys[1], (ROWS, COLS), jnp.float32) ** level_of(part_keys[1], (ROWS, COLS), ((0, 4), (1, 4)), -0.2, 0.2), 0.0, 1.0).astype(jnp.bfloat16)
    kernel_modes = draw_kernel_modes(jax.random.fold_in(key_list[4], 71), part)
    kernel_weight = jnp.clip(jnp.exp(jax.random.uniform(key_list[3], (KERN,), jnp.float32, math.log(0.02), math.log(0.2))), 0.02, 0.2)
    return {"mask_param": mask_param, "target": target, "kernel_modes": kernel_modes, "kernel_weight": kernel_weight}


steepness = 4.0
threshold = 0.4
step_rate = 16.0


def dft_tables():
    frequency = jnp.arange(MODES, dtype=jnp.int32) - MODES // 2
    places = jnp.arange(WIN, dtype=jnp.int32)
    phase_index = jnp.mod(frequency[:, None] * places[None, :], WIN)
    phase_angle = phase_index.astype(jnp.float32) * (2.0 * math.pi / WIN)
    cos_table = jnp.cos(phase_angle).astype(jnp.bfloat16)
    sin_table = jnp.sin(phase_angle).astype(jnp.bfloat16)
    stacked = jnp.concatenate([cos_table, sin_table], axis=0)
    forward_table = jnp.concatenate([cos_table.T, sin_table.T], axis=1)
    inverse_table = jnp.concatenate([jnp.concatenate([cos_table, sin_table], 1), jnp.concatenate([-sin_table, cos_table], 1)], 0)
    adjoint_table = jnp.concatenate([jnp.concatenate([cos_table.T, -sin_table.T], 1), jnp.concatenate([sin_table.T, cos_table.T], 1)], 0)
    return stacked, forward_table, inverse_table, adjoint_table


def window_gradient(window_mask, target_core, weight_core, kernel_modes, kernel_weight):
    stacked, forward_table, inverse_table, adjoint_table = dft_tables()
    half_spec = jnp.dot(window_mask, forward_table, preferred_element_type=jnp.float32).astype(jnp.bfloat16)
    blocks = jnp.dot(stacked, half_spec, preferred_element_type=jnp.float32)
    spec_real = (blocks[:MODES, :MODES] - blocks[MODES:, MODES:]) / (WIN * WIN)
    spec_imag = -(blocks[:MODES, MODES:] + blocks[MODES:, :MODES]) / (WIN * WIN)

    def field_of(kernel_index):
        kernel_one = kernel_modes[kernel_index]
        resp_real = kernel_one[:, :MODES]
        resp_imag = kernel_one[:, MODES:]
        filtered = jnp.concatenate([resp_real * spec_real - resp_imag * spec_imag, resp_real * spec_imag + resp_imag * spec_real], 1).astype(jnp.bfloat16)
        partial_value = jnp.dot(filtered, inverse_table, preferred_element_type=jnp.float32).astype(jnp.bfloat16)
        field_real = partial_value[:, :WIN]
        field_imag = partial_value[:, WIN:]
        rotated = jnp.concatenate([jnp.concatenate([field_real, field_imag], 1), jnp.concatenate([-field_imag, field_real], 1)], 0)
        return jnp.dot(stacked.T, rotated, preferred_element_type=jnp.float32), resp_real, resp_imag

    def add_intensity(running, kernel_index):
        field_pair, resp_real, resp_imag = field_of(kernel_index)
        field_power = field_pair[:, :WIN] * field_pair[:, :WIN] + field_pair[:, WIN:] * field_pair[:, WIN:]
        return running + kernel_weight[kernel_index] * field_power, None

    kernel_ids = jnp.arange(KERN, dtype=jnp.int32)
    intensity, _ = lax.scan(add_intensity, jnp.zeros((WIN, WIN), jnp.float32), kernel_ids)
    core_level = intensity[MARGIN:MARGIN + TILE, MARGIN:MARGIN + TILE]
    printed = jax.nn.sigmoid(steepness * (core_level - threshold))
    core_grad = 2.0 * (printed - target_core.astype(jnp.float32)) * printed * (1.0 - printed) * steepness * weight_core
    grad_full = jnp.pad(core_grad, MARGIN)
    grad_both = jnp.concatenate([grad_full, grad_full], 1)

    def add_adjoint(running, kernel_index):
        field_pair, resp_real, resp_imag = field_of(kernel_index)
        scaled = (field_pair * grad_both * (2.0 * kernel_weight[kernel_index])).astype(jnp.bfloat16)
        half_back = jnp.dot(scaled, adjoint_table, preferred_element_type=jnp.float32).astype(jnp.bfloat16)
        back_modes = jnp.dot(stacked, half_back, preferred_element_type=jnp.float32)
        back_real = back_modes[:MODES, :MODES] + back_modes[MODES:, MODES:]
        back_imag = back_modes[:MODES, MODES:] - back_modes[MODES:, :MODES]
        return (running[0] + resp_real * back_real + resp_imag * back_imag, running[1] + resp_real * back_imag - resp_imag * back_real), None

    zero_modes = jnp.zeros((MODES, MODES), jnp.float32)
    (acc_real, acc_imag), _ = lax.scan(add_adjoint, (zero_modes, zero_modes), kernel_ids)
    combined = jnp.concatenate([acc_real, acc_imag], 1).astype(jnp.bfloat16)
    partial_back = jnp.dot(combined, inverse_table, preferred_element_type=jnp.float32).astype(jnp.bfloat16)
    stacked_back = jnp.concatenate([partial_back[:, :WIN], -partial_back[:, WIN:]], 0)
    mask_grad = jnp.dot(stacked.T, stacked_back, preferred_element_type=jnp.float32) / (WIN * WIN)
    return mask_grad[MARGIN:MARGIN + TILE, MARGIN:MARGIN + TILE]


def tile_join(pieces):
    return pieces.reshape(N_ROW, N_COL, TILE, TILE).transpose(0, 2, 1, 3).reshape(ROWS, COLS)


def reference(mask_param, target, kernel_modes, kernel_weight):
    tile_ids = jnp.arange(N_ROW * N_COL, dtype=jnp.int32)
    soft_mask = jax.nn.sigmoid(mask_param)
    wire_mask = soft_mask.astype(jnp.bfloat16)
    padded = jnp.pad(wire_mask, MARGIN)
    unit_weight = jnp.ones((TILE, TILE), jnp.float32)

    def first_update(tile_index):
        row_start = (tile_index // N_COL) * TILE
        col_start = (tile_index % N_COL) * TILE
        window = lax.dynamic_slice(padded, (row_start, col_start), (WIN, WIN))
        goal_tile = lax.dynamic_slice(target, (row_start, col_start), (TILE, TILE))
        own_soft = lax.dynamic_slice(soft_mask, (row_start, col_start), (TILE, TILE))
        mask_grad = window_gradient(window, goal_tile, unit_weight, kernel_modes, kernel_weight)
        return mask_grad * own_soft * (1.0 - own_soft)

    first_param = mask_param - step_rate * tile_join(lax.map(first_update, tile_ids))
    wire_first = jax.nn.sigmoid(first_param).astype(jnp.bfloat16)
    pad_extra = HALF + MARGIN
    padded_first = jnp.pad(wire_first, ((0, pad_extra), (0, pad_extra)))
    first_padded = jnp.pad(first_param, ((0, HALF), (0, HALF)))
    target_padded = jnp.pad(target, ((0, HALF), (0, HALF)))
    core_place = jnp.arange(TILE, dtype=jnp.int32)

    def second_update(tile_index):
        row_start = (tile_index // N_COL) * TILE
        col_start = (tile_index % N_COL) * TILE
        window = lax.dynamic_slice(padded_first, (row_start + HALF - MARGIN, col_start + HALF - MARGIN), (WIN, WIN))
        goal_tile = lax.dynamic_slice(target_padded, (row_start + HALF, col_start + HALF), (TILE, TILE))
        core_param = lax.dynamic_slice(first_padded, (row_start + HALF, col_start + HALF), (TILE, TILE))
        rows_in = row_start + HALF + core_place < ROWS
        cols_in = col_start + HALF + core_place < COLS
        weight_core = (rows_in[:, None] & cols_in[None, :]).astype(jnp.float32)
        mask_grad = window_gradient(window, goal_tile, weight_core, kernel_modes, kernel_weight)
        core_soft = jax.nn.sigmoid(core_param)
        return core_param - step_rate * (mask_grad * core_soft * (1.0 - core_soft))

    new_cores = tile_join(lax.map(second_update, tile_ids))
    return first_param.at[HALF:, HALF:].set(new_cores[:ROWS - HALF, :COLS - HALF])
```

```python
import functools

import jax
import jax.numpy as jnp
import ml_dtypes
import numpy as np
from jax import lax
from jax.experimental import pallas as pl
from jax.experimental.pallas import tpu as pltpu
from jax.sharding import PartitionSpec as P

TILE = 256
MARGIN = 64
MODES = 64
KERN = 12
HALF = 128
WIN = 384
GRID = 128
PAIR = 2 * MODES

STEEPNESS = 4.0
THRESHOLD = 0.4
STEP = 16.0

MESH = pl.DeviceIdType.MESH
F32 = jnp.float32
BF16 = jnp.bfloat16

AROUND = ((1, 1), (1, -1), (-1, 1), (-1, -1), (1, 0), (-1, 0), (0, 1), (0, -1))
BACK = ((-1, -1), (-1, 0), (0, -1))
AHEAD = ((1, 1), (1, 0), (0, 1))
FIRST_AT = {-1: TILE + MARGIN, 0: MARGIN, 1: MARGIN - TILE}
SECOND_AT = {-1: TILE - MARGIN, 0: -MARGIN}


def cos_sin(places):
    places = np.asarray(places)
    frequency = np.arange(MODES) - MODES // 2
    angle = np.mod(frequency[:, None] * places[None, :], WIN) * (2.0 * np.pi / WIN)
    inside = ((places >= 0) & (places < WIN))[None, :]
    return np.where(inside, np.cos(angle), 0.0), np.where(inside, np.sin(angle), 0.0)


def tables():
    own = np.arange(TILE)

    def columns(offsets):
        parts = [cos_sin(own + offset) for offset in offsets]
        real = [np.concatenate([c.T, -s.T], 1) for c, s in parts]
        imag = [np.concatenate([s.T, c.T], 1) for c, s in parts]
        return np.concatenate(real + imag, 1)

    def rows(offsets):
        parts = [cos_sin(own + offset) for offset in offsets]
        return np.concatenate([np.concatenate([c, -s], 1) for c, s in parts], 0)

    first_at = [FIRST_AT[d] for d in (-1, 0, 1)]
    second_at = [SECOND_AT[d] for d in (-1, 0)]
    c3, s3 = cos_sin(np.arange(GRID) * (WIN // GRID))
    core_c, core_s = cos_sin(own + MARGIN)
    shift = (own + MARGIN)[:, None] / WIN - np.arange(GRID)[None, :] / GRID
    waves = np.arange(1, MODES)[:, None, None] * shift[None]
    resample = (1.0 + 2.0 * np.cos(2.0 * np.pi * waves).sum(0)) / GRID
    made = dict(
        col1=columns(first_at),
        row1=rows(first_at),
        col2=columns(second_at),
        row2=rows(second_at),
        inv3=np.block([[c3, s3], [-s3, c3]]),
        lift=np.concatenate([c3, s3], 0).T,
        up=resample,
        down=resample.T,
        adj=np.block([[c3.T, -s3.T, -s3.T, -c3.T], [s3.T, c3.T, c3.T, -s3.T]]),
        fold=np.concatenate([c3, s3], 1),
        invc=np.block([[core_c, core_s], [-core_s, core_c]]),
        rowc=np.concatenate([core_c.T, -core_s.T], 1),
    )
    held = {name: value.astype(ml_dtypes.bfloat16) for name, value in made.items()}

    def empty(ways, at):
        parts = []
        for di, dj in ways:
            down_c, down_s = (t.sum(1, keepdims=True) for t in cos_sin(own + at[di]))
            over_c, over_s = (t.sum(1)[None] for t in cos_sin(own + at[dj]))
            real = down_c * over_c - down_s * over_s
            imag = -(down_c * over_s + down_s * over_c)
            parts.append(np.concatenate([real, imag], 1) * (-0.5 / (WIN * WIN)))
        return np.stack(parts).astype(np.float32)

    held["none1"] = empty(AROUND, FIRST_AT)
    held["none2"] = empty(BACK, SECOND_AT)
    return held


NAMES = (
    "col1", "row1", "col2", "row2", "inv3", "lift",
    "up", "down", "adj", "fold", "invc", "rowc",
)
ABSENT = ("none1", "none2")


def dot(a, b):
    return jnp.dot(a, b, preferred_element_type=F32)


def above_half(x):
    return 0.5 * jnp.tanh(0.5 * x)


def low_half():
    return lax.broadcasted_iota(jnp.int32, (MODES, PAIR), 1) < MODES


def turned(pair):
    other = pltpu.roll(pair, MODES, 1)
    return jnp.where(low_half(), -other, other)


def spectrum_parts(wire, col, row, count):
    wide = PAIR * count
    half = dot(wire, col[...]).astype(BF16)
    stacked = jnp.concatenate([half[:, :wide], half[:, wide:]], 0)
    return dot(row[...], stacked) * (1.0 / (WIN * WIN))


def adjoint_modes(spec, goal, counted, resp_real, resp_imag, fields, tab):
    filtered = resp_real[...] * spec[None] + resp_imag[...] * turned(spec)[None]
    filtered = filtered.astype(BF16).reshape(KERN * MODES, PAIR)
    spread = dot(filtered, tab["inv3"][...]).astype(BF16)
    level = jnp.zeros((GRID, GRID), F32)
    for k in range(KERN):
        one = spread[k * MODES : (k + 1) * MODES]
        real, imag = one[:, :GRID], one[:, GRID:]
        rotated = jnp.concatenate(
            [one, jnp.concatenate([-imag, real], 1)], 0
        )
        field = dot(tab["lift"][...], rotated)
        fields[k] = field
        level += field[:, :GRID] * field[:, :GRID] + field[:, GRID:] * field[:, GRID:]
    across = dot(level.astype(BF16), tab["down"][...]).astype(BF16)
    core = dot(tab["up"][...], across)
    printed = above_half(STEEPNESS * (core - THRESHOLD))
    pull = (4.0 * STEEPNESS) * (printed + (0.5 - goal.astype(F32))) * (0.25 - printed * printed)
    if counted is not None:
        pull = jnp.where(counted, pull, 0.0)
    pull = dot(pull.astype(BF16), tab["up"][...]).astype(BF16)
    pull = dot(tab["down"][...], pull)
    both = jnp.concatenate([pull, pull], 1)
    scaled = (fields[...] * both[None]).astype(BF16).reshape(KERN * GRID, 2 * GRID)
    back = dot(scaled, tab["adj"][...]).astype(BF16)
    sum_real = jnp.zeros((MODES, PAIR), F32)
    sum_imag = jnp.zeros((MODES, PAIR), F32)
    for k in range(0, KERN, 2):
        one, two = back[k * GRID : (k + 1) * GRID], back[(k + 1) * GRID : (k + 2) * GRID]
        upper = jnp.concatenate([one[:, :PAIR], two[:, :PAIR]], 1)
        lower = jnp.concatenate([one[:, PAIR:], two[:, PAIR:]], 1)
        modes = dot(tab["fold"][...], jnp.concatenate([upper, lower], 0))
        for n in range(2):
            half = modes[:, n * PAIR : (n + 1) * PAIR]
            sum_real += resp_real[k + n] * half
            sum_imag += resp_imag[k + n] * half
    return (sum_real - turned(sum_imag)).astype(BF16)


def core_gradient(modes, tab, low_row, rows, low_col, cols):
    part = jnp.concatenate(
        [
            tab["invc"][:, low_col : low_col + cols],
            tab["invc"][:, TILE + low_col : TILE + low_col + cols],
        ],
        1,
    )
    partial = dot(modes, part).astype(BF16)
    stacked = jnp.concatenate([partial[:, :cols], partial[:, cols:]], 0)
    return dot(tab["rowc"][low_row : low_row + rows], stacked)


def kernel(sizes, weight, *refs):
    count = 3 + len(NAMES)
    far, (none1, none2), refs = refs[:count], refs[count : count + 2], refs[count + 2 :]
    out, near, refs = refs[0], refs[1 : 1 + count], refs[1 + count :]
    mask, target, modes = near[:3]
    tab = dict(zip(NAMES, near[3:]))
    (
        resp_real, resp_imag, fields, first, soft,
        out1, in1, out2, in2, out3, in3, goals,
        send1, recv1, send2, recv2, send3, recv3, send_goal, recv_goal, load, none_sem,
    ) = refs
    n_row, n_col = sizes
    row, col = lax.axis_index("row"), lax.axis_index("col")

    def there(di, dj):
        ok_row = {-1: row >= 1, 0: row >= 0, 1: row < n_row - 1}[di]
        ok_col = {-1: col >= 1, 0: col >= 0, 1: col < n_col - 1}[dj]
        return jnp.logical_and(ok_row, ok_col)

    def place(di, dj):
        return {"row": row + di, "col": col + dj}

    order = ("mask", "col1", "row1", "target", "modes") + NAMES[2:]
    slot = {"mask": 0, "target": 1, "modes": 2} | {n: 3 + k for k, n in enumerate(NAMES)}
    loads = {
        name: pltpu.make_async_copy(far[slot[name]], near[slot[name]], load.at[slot[name]])
        for name in order
    }
    for name in order:
        loads[name].start()

    barrier = pltpu.get_barrier_semaphore()
    for di, dj in AROUND:

        @pl.when(there(di, dj))
        def _():
            pl.semaphore_signal(barrier, inc=1, device_id=place(di, dj), device_id_type=MESH)

    def copies(ways, source, landing, send, recv):
        return [
            pltpu.make_async_remote_copy(
                src_ref=source(n),
                dst_ref=landing.at[n],
                send_sem=send.at[n],
                recv_sem=recv.at[n],
                device_id=place(di, dj),
                device_id_type=MESH,
            )
            for n, (di, dj) in enumerate(ways)
        ]

    def start(ways, group):
        for (di, dj), copy in zip(ways, group):

            @pl.when(there(di, dj))
            def _():
                copy.start()

    def arrive(ways, group):
        for (di, dj), copy in zip(ways, group):

            @pl.when(there(-di, -dj))
            def _():
                copy.wait_recv()

    def sent(ways, group):
        for (di, dj), copy in zip(ways, group):

            @pl.when(there(di, dj))
            def _():
                copy.wait_send()

    def blank(ways, landing):
        for n, (di, dj) in enumerate(ways):

            @pl.when(jnp.logical_not(there(-di, -dj)))
            def _():
                landing[n] = jnp.zeros(landing.shape[1:], landing.dtype)

    def absent(ways, source, landing, sem):
        for n, (di, dj) in enumerate(ways):

            @pl.when(jnp.logical_not(there(-di, -dj)))
            def _():
                copy = pltpu.make_async_copy(source.at[n], landing.at[n], sem.at[n])
                copy.start()
                copy.wait()

    corner = {-1: 0, 0: HALF}
    copies1 = copies(AROUND, lambda n: out1.at[n], in1, send1, recv1)
    copies2 = copies(BACK, lambda n: out2.at[n], in2, send2, recv2)
    copies3 = copies(AHEAD, lambda n: out3, in3, send3, recv3)
    copies_goal = copies(
        BACK,
        lambda n: target.at[
            pl.ds(corner[BACK[n][0]], HALF), pl.ds(corner[BACK[n][1]], HALF)
        ],
        goals,
        send_goal,
        recv_goal,
    )

    for name in ("mask", "col1", "row1"):
        loads[name].wait()
    own_soft = above_half(mask[...])
    soft[...] = own_soft
    parts = spectrum_parts(own_soft.astype(BF16), tab["col1"], tab["row1"], 3)

    def part_of(parts, di, dj):
        return parts[(di + 1) * MODES : (di + 2) * MODES, (dj + 1) * PAIR : (dj + 2) * PAIR]

    for n, (di, dj) in enumerate(AROUND):
        out1[n] = part_of(parts, di, dj).astype(out1.dtype)
    rows_around = 1 + (row >= 1).astype(jnp.int32) + (row < n_row - 1).astype(jnp.int32)
    cols_around = 1 + (col >= 1).astype(jnp.int32) + (col < n_col - 1).astype(jnp.int32)
    pl.semaphore_wait(barrier, rows_around * cols_around - 1)
    start(AROUND, copies1)

    absent(AROUND, none1, in1, none_sem)
    absent(BACK, none2, in2, none_sem)
    blank(AHEAD, in3)
    blank(BACK, goals)
    loads["modes"].wait()
    for k in range(KERN):
        pair = modes[k] * jnp.sqrt(jnp.full((MODES, PAIR), weight[k], F32))
        other = pltpu.roll(pair, MODES, 1)
        resp_real[k] = jnp.where(low_half(), pair, other)
        resp_imag[k] = jnp.where(low_half(), other, pair)

    for name in ("target",) + NAMES[2:]:
        loads[name].wait()
    arrive(AROUND, copies1)
    start(BACK, copies_goal)
    spec = part_of(parts, 0, 0)
    for n in range(len(AROUND)):
        spec += in1[n].astype(F32)
    found = adjoint_modes(spec, target[...], None, resp_real, resp_imag, fields, tab)
    slope = core_gradient(found, tab, 0, TILE, 0, TILE)
    own_soft = soft[...]
    new = mask[...] - (STEP / (WIN * WIN)) * (slope * (0.25 - own_soft * own_soft))
    first[...] = new

    own_soft = above_half(new)
    soft[...] = own_soft
    parts = spectrum_parts(own_soft.astype(BF16), tab["col2"], tab["row2"], 2)
    for n, (di, dj) in enumerate(BACK):
        out2[n] = part_of(parts, di, dj).astype(out2.dtype)
    start(BACK, copies2)
    arrive(BACK, copies_goal)
    goal = jnp.concatenate(
        [
            jnp.concatenate([target[HALF:, HALF:], goals[2]], 1),
            jnp.concatenate([goals[1], goals[0]], 1),
        ],
        0,
    )
    row_at = lax.broadcasted_iota(jnp.int32, (TILE, TILE), 0)
    col_at = lax.broadcasted_iota(jnp.int32, (TILE, TILE), 1)
    row_end = jnp.where(row < n_row - 1, TILE, HALF)
    col_end = jnp.where(col < n_col - 1, TILE, HALF)
    counted = jnp.logical_and(row_at < row_end, col_at < col_end)
    arrive(BACK, copies2)
    spec = part_of(parts, 0, 0)
    for n in range(len(BACK)):
        spec += in2[n].astype(F32)
    found = adjoint_modes(spec, goal, counted, resp_real, resp_imag, fields, tab)
    out3[...] = found
    start(AHEAD, copies3)

    def finish(modes, di, dj):
        at_row, at_col = (0 if di else HALF), (0 if dj else HALF)
        slope = core_gradient(modes, tab, HALF - at_row, HALF, HALF - at_col, HALF)
        here = (slice(at_row, at_row + HALF), slice(at_col, at_col + HALF))
        own_soft, before = soft[here], first[here]
        after = before - (STEP / (WIN * WIN)) * (slope * (0.25 - own_soft * own_soft))
        out[here] = jnp.where(there(-di, -dj), after, before)

    finish(found, 0, 0)
    arrive(AHEAD, copies3)
    for n, (di, dj) in enumerate(AHEAD):
        finish(in3[n], di, dj)

    sent(AROUND, copies1)
    sent(BACK, copies_goal)
    sent(BACK, copies2)
    sent(AHEAD, copies3)


def solution(mesh):
    sizes = (mesh.shape["row"], mesh.shape["col"])
    made = tables()
    held = [made[name] for name in NAMES + ABSENT]

    def per_device(mask_param, target, kernel_modes, kernel_weight):
        vmem = pl.BlockSpec(memory_space=pltpu.VMEM)
        message = (MODES, PAIR)
        return pl.pallas_call(
            functools.partial(kernel, sizes),
            out_shape=jax.ShapeDtypeStruct((TILE, TILE), F32),
            in_specs=[pl.BlockSpec(memory_space=pltpu.SMEM)]
            + [pl.BlockSpec(memory_space=pltpu.HBM)] * (3 + len(held)),
            out_specs=vmem,
            scratch_shapes=[
                pltpu.VMEM((TILE, TILE), F32),
                pltpu.VMEM((TILE, TILE), BF16),
                pltpu.VMEM((KERN,) + message, F32),
            ]
            + [pltpu.VMEM(made[name].shape, BF16) for name in NAMES]
            + [
                pltpu.VMEM((KERN,) + message, F32),
                pltpu.VMEM((KERN,) + message, F32),
                pltpu.VMEM((KERN, GRID, 2 * GRID), F32),
                pltpu.VMEM((TILE, TILE), F32),
                pltpu.VMEM((TILE, TILE), F32),
                pltpu.VMEM((len(AROUND),) + message, F32),
                pltpu.VMEM((len(AROUND),) + message, F32),
                pltpu.VMEM((len(BACK),) + message, F32),
                pltpu.VMEM((len(BACK),) + message, F32),
                pltpu.VMEM(message, BF16),
                pltpu.VMEM((len(AHEAD),) + message, BF16),
                pltpu.VMEM((len(BACK), HALF, HALF), BF16),
            ]
            + [
                pltpu.SemaphoreType.DMA((count,))
                for count in (8, 8, 3, 3, 3, 3, 3, 3, 3 + len(NAMES), 8)
            ],
            compiler_params=pltpu.CompilerParams(
                collective_id=0, has_side_effects=True, vmem_limit_bytes=60 * 1024 * 1024
            ),
            cost_estimate=pl.CostEstimate(
                flops=1_000_000_000, bytes_accessed=3_000_000, transcendentals=300_000
            ),
        )(kernel_weight, mask_param, target, kernel_modes, *[jnp.asarray(t) for t in held])

    spread = P(("grp", "row"), "col")
    return jax.shard_map(
        per_device, mesh=mesh, in_specs=(spread, spread, P(), P()), out_specs=spread,
        check_vma=False,
    )
```

```python
import functools

import jax
import jax.numpy as jnp
import ml_dtypes
import numpy as np
from jax import lax
from jax.experimental import pallas as pl
from jax.experimental.pallas import tpu as pltpu
from jax.sharding import PartitionSpec as P

TILE = 256
MARGIN = 64
MODES = 64
KERN = 12
HALF = 128
WIN = 384
GRID = 128
PAIR = 2 * MODES

STEEPNESS = 4.0
THRESHOLD = 0.4
STEP = 16.0

MESH = pl.DeviceIdType.MESH
F32 = jnp.float32
BF16 = jnp.bfloat16

AROUND = ((1, 1), (1, -1), (-1, 1), (-1, -1), (1, 0), (-1, 0), (0, 1), (0, -1))
BACK = ((-1, -1), (-1, 0), (0, -1))
AHEAD = ((1, 1), (1, 0), (0, 1))
FIRST_AT = {-1: TILE + MARGIN, 0: MARGIN, 1: MARGIN - TILE}
SECOND_AT = {-1: TILE - MARGIN, 0: -MARGIN}


def cos_sin(places):
    places = np.asarray(places)
    frequency = np.arange(MODES) - MODES // 2
    angle = np.mod(frequency[:, None] * places[None, :], WIN) * (2.0 * np.pi / WIN)
    inside = ((places >= 0) & (places < WIN))[None, :]
    return np.where(inside, np.cos(angle), 0.0), np.where(inside, np.sin(angle), 0.0)


def tables():
    own = np.arange(TILE)

    def columns(offsets):
        parts = [cos_sin(own + offset) for offset in offsets]
        real = [np.concatenate([c.T, -s.T], 1) for c, s in parts]
        imag = [np.concatenate([s.T, c.T], 1) for c, s in parts]
        return np.concatenate(real + imag, 1)

    def rows(offsets):
        parts = [cos_sin(own + offset) for offset in offsets]
        return np.concatenate([np.concatenate([c, -s], 1) for c, s in parts], 0)

    first_at = [FIRST_AT[d] for d in (-1, 0, 1)]
    second_at = [SECOND_AT[d] for d in (-1, 0)]
    c3, s3 = cos_sin(np.arange(GRID) * (WIN // GRID))
    core_c, core_s = cos_sin(own + MARGIN)
    shift = (own + MARGIN)[:, None] / WIN - np.arange(GRID)[None, :] / GRID
    waves = np.arange(1, MODES)[:, None, None] * shift[None]
    resample = (1.0 + 2.0 * np.cos(2.0 * np.pi * waves).sum(0)) / GRID
    made = dict(
        col1=columns(first_at),
        row1=rows(first_at),
        col2=columns(second_at),
        row2=rows(second_at),
        inv3=np.block([[c3, s3], [-s3, c3]]),
        lift=np.concatenate([c3, s3], 0).T,
        up=resample,
        down=resample.T,
        adj=np.block([[c3.T, -s3.T, -s3.T, -c3.T], [s3.T, c3.T, c3.T, -s3.T]]),
        fold=np.concatenate([c3, s3], 1),
        invc=np.block([[core_c, core_s], [-core_s, core_c]]),
        rowc=np.concatenate([core_c.T, -core_s.T], 1),
    )
    held = {name: value.astype(ml_dtypes.bfloat16) for name, value in made.items()}

    def minus_half(di, dj, at):
        down_c, down_s = (t.sum(1, keepdims=True) for t in cos_sin(own + at[di]))
        over_c, over_s = (t.sum(1)[None] for t in cos_sin(own + at[dj]))
        real = down_c * over_c - down_s * over_s
        imag = -(down_c * over_s + down_s * over_c)
        return np.concatenate([real, imag], 1) * (-0.5 / (WIN * WIN))

    def empty(ways, at, states, missing):
        made = []
        for state in range(states):
            total = np.zeros((MODES, PAIR))
            for di, dj in ways:
                if missing(state, di, dj):
                    total += minus_half(di, dj, at)
            made.append(total)
        return np.stack(made).astype(np.float32)

    held["none1"] = empty(
        AROUND,
        FIRST_AT,
        16,
        lambda n, di, dj: (
            (di > 0 and n & 1) or (di < 0 and n & 2) or (dj > 0 and n & 4) or (dj < 0 and n & 8)
        ),
    )
    held["none2"] = empty(
        BACK, SECOND_AT, 4, lambda n, di, dj: (di < 0 and n & 1) or (dj < 0 and n & 2)
    )
    return held


NAMES = (
    "col1", "row1", "col2", "row2", "inv3", "lift",
    "up", "down", "adj", "fold", "invc", "rowc",
)
ABSENT = ("none1", "none2")


def dot(a, b):
    return jnp.dot(a, b, preferred_element_type=F32)


def above_half(x):
    return 0.5 * jnp.tanh(0.5 * x)


def low_half():
    return lax.broadcasted_iota(jnp.int32, (MODES, PAIR), 1) < MODES


def turned(pair):
    other = pltpu.roll(pair, MODES, 1)
    return jnp.where(low_half(), -other, other)


def spectrum_parts(wire, col, row, count):
    wide = PAIR * count
    half = dot(wire, col[...]).astype(BF16)
    stacked = jnp.concatenate([half[:, :wide], half[:, wide:]], 0)
    return dot(row[...], stacked) * (1.0 / (WIN * WIN))


def adjoint_modes(spec, goal, counted, resp_real, resp_imag, fields, tab):
    filtered = resp_real[...] * spec[None] + resp_imag[...] * turned(spec)[None]
    filtered = filtered.astype(BF16).reshape(KERN * MODES, PAIR)
    spread = dot(filtered, tab["inv3"][...]).astype(BF16)
    level = jnp.zeros((GRID, GRID), F32)
    for k in range(KERN):
        one = spread[k * MODES : (k + 1) * MODES]
        real, imag = one[:, :GRID], one[:, GRID:]
        rotated = jnp.concatenate(
            [one, jnp.concatenate([-imag, real], 1)], 0
        )
        field = dot(tab["lift"][...], rotated)
        fields[k] = field.astype(BF16)
        level += field[:, :GRID] * field[:, :GRID] + field[:, GRID:] * field[:, GRID:]
    across = dot(level.astype(BF16), tab["down"][...]).astype(BF16)
    core = dot(tab["up"][...], across)
    printed = above_half(STEEPNESS * (core - THRESHOLD))
    pull = (4.0 * STEEPNESS) * (printed + (0.5 - goal.astype(F32))) * (0.25 - printed * printed)
    if counted is not None:
        pull = jnp.where(counted, pull, 0.0)
    pull = dot(pull.astype(BF16), tab["up"][...]).astype(BF16)
    pull = dot(tab["down"][...], pull)
    pull = pull.astype(BF16)
    both = jnp.concatenate([pull, pull], 1)
    scaled = (fields[...] * both[None]).reshape(KERN * GRID, 2 * GRID)
    back = dot(scaled, tab["adj"][...]).astype(BF16)
    sum_real = jnp.zeros((MODES, PAIR), F32)
    sum_imag = jnp.zeros((MODES, PAIR), F32)
    for k in range(0, KERN, 2):
        one, two = back[k * GRID : (k + 1) * GRID], back[(k + 1) * GRID : (k + 2) * GRID]
        upper = jnp.concatenate([one[:, :PAIR], two[:, :PAIR]], 1)
        lower = jnp.concatenate([one[:, PAIR:], two[:, PAIR:]], 1)
        modes = dot(tab["fold"][...], jnp.concatenate([upper, lower], 0))
        for n in range(2):
            half = modes[:, n * PAIR : (n + 1) * PAIR]
            sum_real += resp_real[k + n] * half
            sum_imag += resp_imag[k + n] * half
    return (sum_real - turned(sum_imag)).astype(BF16)


def core_gradient(modes, tab, low_row, rows, low_col, cols):
    part = jnp.concatenate(
        [
            tab["invc"][:, low_col : low_col + cols],
            tab["invc"][:, TILE + low_col : TILE + low_col + cols],
        ],
        1,
    )
    partial = dot(modes, part).astype(BF16)
    stacked = jnp.concatenate([partial[:, :cols], partial[:, cols:]], 0)
    return dot(tab["rowc"][low_row : low_row + rows], stacked)


def kernel(sizes, weight, *refs):
    count = 3 + len(NAMES)
    far, (none1, none2), refs = refs[:count], refs[count : count + 2], refs[count + 2 :]
    out, near, refs = refs[0], refs[1 : 1 + count], refs[1 + count :]
    mask, target, modes = near[:3]
    tab = dict(zip(NAMES, near[3:]))
    (
        resp_real, resp_imag, fields, first, soft,
        out1, in1, out2, in2, out3, in3, goals, base1, base2,
        send1, recv1, send2, recv2, send3, recv3, send_goal, recv_goal, load, none_sem,
    ) = refs
    n_row, n_col = sizes
    row, col = lax.axis_index("row"), lax.axis_index("col")

    def there(di, dj):
        ok_row = {-1: row >= 1, 0: row >= 0, 1: row < n_row - 1}[di]
        ok_col = {-1: col >= 1, 0: col >= 0, 1: col < n_col - 1}[dj]
        return jnp.logical_and(ok_row, ok_col)

    def place(di, dj):
        return {"row": row + di, "col": col + dj}

    order = ("mask", "col1", "row1", "target", "modes") + NAMES[2:]
    slot = {"mask": 0, "target": 1, "modes": 2} | {n: 3 + k for k, n in enumerate(NAMES)}
    loads = {
        name: pltpu.make_async_copy(far[slot[name]], near[slot[name]], load.at[slot[name]])
        for name in order
    }
    for name in order:
        loads[name].start()
    edges = [(row == 0), (row == n_row - 1), (col == 0), (col == n_col - 1)]
    up, down, left, right = [edge.astype(jnp.int32) for edge in edges]
    load_none1 = pltpu.make_async_copy(
        none1.at[up + 2 * down + 4 * left + 8 * right], base1, none_sem.at[0]
    )
    load_none2 = pltpu.make_async_copy(none2.at[down + 2 * right], base2, none_sem.at[1])
    load_none1.start()
    load_none2.start()

    barrier = pltpu.get_barrier_semaphore()
    for di, dj in AROUND:

        @pl.when(there(di, dj))
        def _():
            pl.semaphore_signal(barrier, inc=1, device_id=place(di, dj), device_id_type=MESH)

    def copies(ways, source, landing, send, recv):
        return [
            pltpu.make_async_remote_copy(
                src_ref=source(n),
                dst_ref=landing.at[n],
                send_sem=send.at[n],
                recv_sem=recv.at[n],
                device_id=place(di, dj),
                device_id_type=MESH,
            )
            for n, (di, dj) in enumerate(ways)
        ]

    def start(ways, group):
        for (di, dj), copy in zip(ways, group):

            @pl.when(there(di, dj))
            def _():
                copy.start()

    def arrive(ways, group):
        for (di, dj), copy in zip(ways, group):

            @pl.when(there(-di, -dj))
            def _():
                copy.wait_recv()

    def sent(ways, group):
        for (di, dj), copy in zip(ways, group):

            @pl.when(there(di, dj))
            def _():
                copy.wait_send()

    def blank(ways, landing):
        for n, (di, dj) in enumerate(ways):

            @pl.when(jnp.logical_not(there(-di, -dj)))
            def _():
                landing[n] = jnp.zeros(landing.shape[1:], landing.dtype)

    corner = {-1: 0, 0: HALF}
    copies1 = copies(AROUND, lambda n: out1.at[n], in1, send1, recv1)
    copies2 = copies(BACK, lambda n: out2.at[n], in2, send2, recv2)
    copies3 = copies(AHEAD, lambda n: out3, in3, send3, recv3)
    copies_goal = copies(
        BACK,
        lambda n: target.at[
            pl.ds(corner[BACK[n][0]], HALF), pl.ds(corner[BACK[n][1]], HALF)
        ],
        goals,
        send_goal,
        recv_goal,
    )

    for name in ("mask", "col1", "row1"):
        loads[name].wait()
    own_soft = above_half(mask[...])
    soft[...] = own_soft
    parts = spectrum_parts(own_soft.astype(BF16), tab["col1"], tab["row1"], 3)

    def part_of(parts, di, dj):
        return parts[(di + 1) * MODES : (di + 2) * MODES, (dj + 1) * PAIR : (dj + 2) * PAIR]

    for n, (di, dj) in enumerate(AROUND):
        out1[n] = part_of(parts, di, dj).astype(out1.dtype)
    rows_around = 1 + (row >= 1).astype(jnp.int32) + (row < n_row - 1).astype(jnp.int32)
    cols_around = 1 + (col >= 1).astype(jnp.int32) + (col < n_col - 1).astype(jnp.int32)
    pl.semaphore_wait(barrier, rows_around * cols_around - 1)
    start(AROUND, copies1)

    blank(AROUND, in1)
    blank(BACK, in2)
    blank(AHEAD, in3)
    blank(BACK, goals)
    loads["modes"].wait()
    for k in range(KERN):
        pair = modes[k] * jnp.sqrt(jnp.full((MODES, PAIR), weight[k], F32))
        other = pltpu.roll(pair, MODES, 1)
        resp_real[k] = jnp.where(low_half(), pair, other)
        resp_imag[k] = jnp.where(low_half(), other, pair)

    for name in ("target",) + NAMES[2:]:
        loads[name].wait()
    load_none1.wait()
    load_none2.wait()
    arrive(AROUND, copies1)
    start(BACK, copies_goal)
    spec = part_of(parts, 0, 0) + base1[...]
    for n in range(len(AROUND)):
        spec += in1[n].astype(F32)
    found = adjoint_modes(spec, target[...], None, resp_real, resp_imag, fields, tab)
    slope = core_gradient(found, tab, 0, TILE, 0, TILE)
    own_soft = soft[...]
    new = mask[...] - (STEP / (WIN * WIN)) * (slope * (0.25 - own_soft * own_soft))
    first[...] = new

    own_soft = above_half(new)
    soft[...] = own_soft
    parts = spectrum_parts(own_soft.astype(BF16), tab["col2"], tab["row2"], 2)
    for n, (di, dj) in enumerate(BACK):
        out2[n] = part_of(parts, di, dj).astype(out2.dtype)
    start(BACK, copies2)
    arrive(BACK, copies_goal)
    goal = jnp.concatenate(
        [
            jnp.concatenate([target[HALF:, HALF:], goals[2]], 1),
            jnp.concatenate([goals[1], goals[0]], 1),
        ],
        0,
    )
    row_at = lax.broadcasted_iota(jnp.int32, (TILE, TILE), 0)
    col_at = lax.broadcasted_iota(jnp.int32, (TILE, TILE), 1)
    row_end = jnp.where(row < n_row - 1, TILE, HALF)
    col_end = jnp.where(col < n_col - 1, TILE, HALF)
    counted = jnp.logical_and(row_at < row_end, col_at < col_end)
    arrive(BACK, copies2)
    spec = part_of(parts, 0, 0) + base2[...]
    for n in range(len(BACK)):
        spec += in2[n].astype(F32)
    found = adjoint_modes(spec, goal, counted, resp_real, resp_imag, fields, tab)
    out3[...] = found
    start(AHEAD, copies3)

    def finish(modes, di, dj):
        at_row, at_col = (0 if di else HALF), (0 if dj else HALF)
        slope = core_gradient(modes, tab, HALF - at_row, HALF, HALF - at_col, HALF)
        here = (slice(at_row, at_row + HALF), slice(at_col, at_col + HALF))
        own_soft, before = soft[here], first[here]
        after = before - (STEP / (WIN * WIN)) * (slope * (0.25 - own_soft * own_soft))
        out[here] = jnp.where(there(-di, -dj), after, before)

    finish(found, 0, 0)
    arrive(AHEAD, copies3)
    for n, (di, dj) in enumerate(AHEAD):
        finish(in3[n], di, dj)

    sent(AROUND, copies1)
    sent(BACK, copies_goal)
    sent(BACK, copies2)
    sent(AHEAD, copies3)


def solution(mesh):
    sizes = (mesh.shape["row"], mesh.shape["col"])
    made = tables()
    held = [made[name] for name in NAMES + ABSENT]

    def per_device(mask_param, target, kernel_modes, kernel_weight):
        vmem = pl.BlockSpec(memory_space=pltpu.VMEM)
        message = (MODES, PAIR)
        return pl.pallas_call(
            functools.partial(kernel, sizes),
            out_shape=jax.ShapeDtypeStruct((TILE, TILE), F32),
            in_specs=[pl.BlockSpec(memory_space=pltpu.SMEM)]
            + [pl.BlockSpec(memory_space=pltpu.HBM)] * (3 + len(held)),
            out_specs=vmem,
            scratch_shapes=[
                pltpu.VMEM((TILE, TILE), F32),
                pltpu.VMEM((TILE, TILE), BF16),
                pltpu.VMEM((KERN,) + message, F32),
            ]
            + [pltpu.VMEM(made[name].shape, BF16) for name in NAMES]
            + [
                pltpu.VMEM((KERN,) + message, F32),
                pltpu.VMEM((KERN,) + message, F32),
                pltpu.VMEM((KERN, GRID, 2 * GRID), BF16),
                pltpu.VMEM((TILE, TILE), F32),
                pltpu.VMEM((TILE, TILE), F32),
                pltpu.VMEM((len(AROUND),) + message, BF16),
                pltpu.VMEM((len(AROUND),) + message, BF16),
                pltpu.VMEM((len(BACK),) + message, BF16),
                pltpu.VMEM((len(BACK),) + message, BF16),
                pltpu.VMEM(message, BF16),
                pltpu.VMEM((len(AHEAD),) + message, BF16),
                pltpu.VMEM((len(BACK), HALF, HALF), BF16),
                pltpu.VMEM(message, F32),
                pltpu.VMEM(message, F32),
            ]
            + [
                pltpu.SemaphoreType.DMA((count,))
                for count in (8, 8, 3, 3, 3, 3, 3, 3, 3 + len(NAMES), 2)
            ],
            compiler_params=pltpu.CompilerParams(
                collective_id=0, has_side_effects=True, vmem_limit_bytes=60 * 1024 * 1024
            ),
            cost_estimate=pl.CostEstimate(
                flops=1_000_000_000, bytes_accessed=3_000_000, transcendentals=300_000
            ),
        )(kernel_weight, mask_param, target, kernel_modes, *[jnp.asarray(t) for t in held])

    spread = P(("grp", "row"), "col")
    return jax.shard_map(
        per_device, mesh=mesh, in_specs=(spread, spread, P(), P()), out_specs=spread,
        check_vma=False,
    )
```

```python
import functools

import jax
import jax.numpy as jnp
import ml_dtypes
import numpy as np
from jax import lax
from jax.experimental import pallas as pl
from jax.experimental.pallas import tpu as pltpu
from jax.sharding import PartitionSpec as P

TILE = 256
MARGIN = 64
MODES = 64
KERN = 12
HALF = 128
WIN = 384
GRID = 128
PAIR = 2 * MODES
GROUP = 4

STEEPNESS = 4.0
THRESHOLD = 0.4
STEP = 16.0

MESH = pl.DeviceIdType.MESH
F32 = jnp.float32
BF16 = jnp.bfloat16

AROUND = ((1, 1), (1, -1), (-1, 1), (-1, -1), (1, 0), (-1, 0), (0, 1), (0, -1))
BACK = ((-1, -1), (-1, 0), (0, -1))
AHEAD = ((1, 1), (1, 0), (0, 1))
FIRST_AT = {-1: TILE + MARGIN, 0: MARGIN, 1: MARGIN - TILE}
SECOND_AT = {-1: TILE - MARGIN, 0: -MARGIN}


def cos_sin(places):
    places = np.asarray(places)
    frequency = np.arange(MODES) - MODES // 2
    angle = np.mod(frequency[:, None] * places[None, :], WIN) * (2.0 * np.pi / WIN)
    inside = ((places >= 0) & (places < WIN))[None, :]
    return np.where(inside, np.cos(angle), 0.0), np.where(inside, np.sin(angle), 0.0)


def tables():
    own = np.arange(TILE)

    def columns(offsets):
        parts = [cos_sin(own + offset) for offset in offsets]
        real = [np.concatenate([c.T, -s.T], 1) for c, s in parts]
        imag = [np.concatenate([s.T, c.T], 1) for c, s in parts]
        return np.concatenate(real + imag, 1)

    def rows(offsets):
        parts = [cos_sin(own + offset) for offset in offsets]
        return np.concatenate([np.concatenate([c, -s], 1) for c, s in parts], 0)

    first_at = [FIRST_AT[d] for d in (-1, 0, 1)]
    second_at = [SECOND_AT[d] for d in (-1, 0)]
    c3, s3 = cos_sin(np.arange(GRID) * (WIN // GRID))
    core_c, core_s = cos_sin(own + MARGIN)
    shift = (own + MARGIN)[:, None] / WIN - np.arange(GRID)[None, :] / GRID
    waves = np.arange(1, MODES)[:, None, None] * shift[None]
    resample = (1.0 + 2.0 * np.cos(2.0 * np.pi * waves).sum(0)) / GRID
    made = dict(
        col1=columns(first_at),
        row1=rows(first_at),
        col2=columns(second_at),
        row2=rows(second_at),
        inv3=np.block([[c3, s3], [-s3, c3]]),
        lift=np.concatenate([c3, s3], 0).T,
        up=resample,
        down=resample.T,
        adj=np.block([[c3.T, -s3.T, -s3.T, -c3.T], [s3.T, c3.T, c3.T, -s3.T]]),
        fold=np.concatenate([c3, s3], 1),
        invc=np.block([[core_c, core_s], [-core_s, core_c]]),
        rowc=np.concatenate([core_c.T, -core_s.T], 1),
    )
    held = {name: value.astype(ml_dtypes.bfloat16) for name, value in made.items()}

    def minus_half(di, dj, at):
        down_c, down_s = (t.sum(1, keepdims=True) for t in cos_sin(own + at[di]))
        over_c, over_s = (t.sum(1)[None] for t in cos_sin(own + at[dj]))
        real = down_c * over_c - down_s * over_s
        imag = -(down_c * over_s + down_s * over_c)
        return np.concatenate([real, imag], 1) * (-0.5 / (WIN * WIN))

    def empty(ways, at, states, missing):
        made = []
        for state in range(states):
            total = np.zeros((MODES, PAIR))
            for di, dj in ways:
                if missing(state, di, dj):
                    total += minus_half(di, dj, at)
            made.append(total)
        return np.stack(made).astype(np.float32)

    held["none1"] = empty(
        AROUND,
        FIRST_AT,
        16,
        lambda n, di, dj: (
            (di > 0 and n & 1) or (di < 0 and n & 2) or (dj > 0 and n & 4) or (dj < 0 and n & 8)
        ),
    )
    held["none2"] = empty(
        BACK, SECOND_AT, 4, lambda n, di, dj: (di < 0 and n & 1) or (dj < 0 and n & 2)
    )
    return held


NAMES = (
    "col1", "row1", "col2", "row2", "inv3", "lift",
    "up", "down", "adj", "fold", "invc", "rowc",
)
ABSENT = ("none1", "none2")


def dot(a, b):
    return jnp.dot(a, b, preferred_element_type=F32)


def above_half(x):
    return 0.5 * jnp.tanh(0.5 * x)


def low_half():
    return lax.broadcasted_iota(jnp.int32, (MODES, PAIR), 1) < MODES


def turned(pair):
    other = pltpu.roll(pair, MODES, 1)
    return jnp.where(low_half(), -other, other)


def spectrum_parts(wire, col, row, count):
    wide = PAIR * count
    half = dot(wire, col[...]).astype(BF16)
    stacked = jnp.concatenate([half[:, :wide], half[:, wide:]], 0)
    return dot(row[...], stacked) * (1.0 / (WIN * WIN))


def adjoint_modes(spec, goal, counted, resp_real, resp_imag, fields, tab):
    other = turned(spec)
    lifted = []
    for k in range(0, KERN, 2):
        pair = []
        for n in (k, k + 1):
            filtered = resp_real[n] * spec + resp_imag[n] * other
            rotated = resp_real[n] * other - resp_imag[n] * spec
            pair.append(jnp.concatenate([filtered.astype(BF16), rotated.astype(BF16)], 0))
        both = dot(tab["lift"][...], jnp.concatenate(pair, 1)).astype(BF16)
        lifted += [both[:, :PAIR], both[:, PAIR:]]
    level = jnp.zeros((GRID, GRID), F32)
    for k in range(0, KERN, GROUP):
        group = dot(jnp.concatenate(lifted[k : k + GROUP], 0), tab["inv3"][...])
        for n in range(GROUP):
            field = group[n * GRID : (n + 1) * GRID]
            fields[k + n] = field.astype(BF16)
            level += field[:, :GRID] * field[:, :GRID] + field[:, GRID:] * field[:, GRID:]
    across = dot(level.astype(BF16), tab["down"][...]).astype(BF16)
    core = dot(tab["up"][...], across)
    printed = above_half(STEEPNESS * (core - THRESHOLD))
    pull = (4.0 * STEEPNESS) * (printed + (0.5 - goal.astype(F32))) * (0.25 - printed * printed)
    if counted is not None:
        pull = jnp.where(counted, pull, 0.0)
    pull = dot(pull.astype(BF16), tab["up"][...]).astype(BF16)
    pull = dot(tab["down"][...], pull)
    pull = pull.astype(BF16)
    both = jnp.concatenate([pull, pull], 1)
    scaled = (fields[...] * both[None]).reshape(KERN * GRID, 2 * GRID)
    back = dot(scaled, tab["adj"][...]).astype(BF16)
    sum_real = jnp.zeros((MODES, PAIR), F32)
    sum_imag = jnp.zeros((MODES, PAIR), F32)
    for k in range(0, KERN, 2):
        one, two = back[k * GRID : (k + 1) * GRID], back[(k + 1) * GRID : (k + 2) * GRID]
        upper = jnp.concatenate([one[:, :PAIR], two[:, :PAIR]], 1)
        lower = jnp.concatenate([one[:, PAIR:], two[:, PAIR:]], 1)
        modes = dot(tab["fold"][...], jnp.concatenate([upper, lower], 0))
        for n in range(2):
            half = modes[:, n * PAIR : (n + 1) * PAIR]
            sum_real += resp_real[k + n] * half
            sum_imag += resp_imag[k + n] * half
    return (sum_real - turned(sum_imag)).astype(BF16)


def core_gradient(modes, tab, low_row, rows, low_col, cols):
    part = jnp.concatenate(
        [
            tab["invc"][:, low_col : low_col + cols],
            tab["invc"][:, TILE + low_col : TILE + low_col + cols],
        ],
        1,
    )
    partial = dot(modes, part).astype(BF16)
    stacked = jnp.concatenate([partial[:, :cols], partial[:, cols:]], 0)
    return dot(tab["rowc"][low_row : low_row + rows], stacked)


def kernel(sizes, weight, *refs):
    count = 3 + len(NAMES)
    far, (none1, none2), refs = refs[:count], refs[count : count + 2], refs[count + 2 :]
    out, near, refs = refs[0], refs[1 : 1 + count], refs[1 + count :]
    mask, target, modes = near[:3]
    tab = dict(zip(NAMES, near[3:]))
    (
        resp_real, resp_imag, fields, first, soft,
        out1, in1, out2, in2, out3, in3, goals, base1, base2,
        send1, recv1, send2, recv2, send3, recv3, send_goal, recv_goal, load, none_sem,
        moved, save,
    ) = refs
    n_row, n_col = sizes
    row, col = lax.axis_index("row"), lax.axis_index("col")

    def there(di, dj):
        ok_row = {-1: row >= 1, 0: row >= 0, 1: row < n_row - 1}[di]
        ok_col = {-1: col >= 1, 0: col >= 0, 1: col < n_col - 1}[dj]
        return jnp.logical_and(ok_row, ok_col)

    def place(di, dj):
        return {"row": row + di, "col": col + dj}

    barrier = pltpu.get_barrier_semaphore()
    for di, dj in AROUND:

        @pl.when(there(di, dj))
        def _():
            pl.semaphore_signal(barrier, inc=1, device_id=place(di, dj), device_id_type=MESH)

    order = ("mask", "col1", "row1", "target", "modes") + NAMES[2:]
    slot = {"mask": 0, "target": 1, "modes": 2} | {n: 3 + k for k, n in enumerate(NAMES)}
    loads = {
        name: pltpu.make_async_copy(far[slot[name]], near[slot[name]], load.at[slot[name]])
        for name in order
    }
    for name in order:
        loads[name].start()
    edges = [(row == 0), (row == n_row - 1), (col == 0), (col == n_col - 1)]
    up, down, left, right = [edge.astype(jnp.int32) for edge in edges]
    load_none1 = pltpu.make_async_copy(
        none1.at[up + 2 * down + 4 * left + 8 * right], base1, none_sem.at[0]
    )
    load_none2 = pltpu.make_async_copy(none2.at[down + 2 * right], base2, none_sem.at[1])
    load_none1.start()
    load_none2.start()

    def copies(ways, source, landing, send, recv):
        return [
            pltpu.make_async_remote_copy(
                src_ref=source(n),
                dst_ref=landing.at[n],
                send_sem=send.at[n],
                recv_sem=recv.at[n],
                device_id=place(di, dj),
                device_id_type=MESH,
            )
            for n, (di, dj) in enumerate(ways)
        ]

    def start(ways, group):
        for (di, dj), copy in zip(ways, group):

            @pl.when(there(di, dj))
            def _():
                copy.start()

    def arrive(ways, group):
        for (di, dj), copy in zip(ways, group):

            @pl.when(there(-di, -dj))
            def _():
                copy.wait_recv()

    def sent(ways, group):
        for (di, dj), copy in zip(ways, group):

            @pl.when(there(di, dj))
            def _():
                copy.wait_send()

    def blank(ways, landing):
        for n, (di, dj) in enumerate(ways):

            @pl.when(jnp.logical_not(there(-di, -dj)))
            def _():
                landing[n] = jnp.zeros(landing.shape[1:], landing.dtype)

    corner = {-1: 0, 0: HALF}
    copies1 = copies(AROUND, lambda n: out1.at[n], in1, send1, recv1)
    copies2 = copies(BACK, lambda n: out2.at[n], in2, send2, recv2)
    copies3 = copies(AHEAD, lambda n: out3, in3, send3, recv3)
    copies_goal = copies(
        BACK,
        lambda n: target.at[
            pl.ds(corner[BACK[n][0]], HALF), pl.ds(corner[BACK[n][1]], HALF)
        ],
        goals,
        send_goal,
        recv_goal,
    )

    for name in ("mask", "col1", "row1"):
        loads[name].wait()
    own_soft = above_half(mask[...])
    soft[...] = own_soft
    parts = spectrum_parts(own_soft.astype(BF16), tab["col1"], tab["row1"], 3)

    def part_of(parts, di, dj):
        return parts[(di + 1) * MODES : (di + 2) * MODES, (dj + 1) * PAIR : (dj + 2) * PAIR]

    for n, (di, dj) in enumerate(AROUND):
        out1[n] = part_of(parts, di, dj).astype(out1.dtype)
    rows_around = 1 + (row >= 1).astype(jnp.int32) + (row < n_row - 1).astype(jnp.int32)
    cols_around = 1 + (col >= 1).astype(jnp.int32) + (col < n_col - 1).astype(jnp.int32)
    pl.semaphore_wait(barrier, rows_around * cols_around - 1)
    start(AROUND, copies1)

    blank(AROUND, in1)
    blank(BACK, in2)
    blank(AHEAD, in3)
    blank(BACK, goals)
    loads["modes"].wait()
    for k in range(KERN):
        pair = modes[k] * jnp.sqrt(jnp.full((MODES, PAIR), weight[k], F32))
        other = pltpu.roll(pair, MODES, 1)
        resp_real[k] = jnp.where(low_half(), pair, other)
        resp_imag[k] = jnp.where(low_half(), other, pair)

    for name in ("target",) + NAMES[2:]:
        loads[name].wait()
    load_none1.wait()
    load_none2.wait()
    arrive(AROUND, copies1)
    start(BACK, copies_goal)
    spec = part_of(parts, 0, 0) + base1[...]
    for n in range(len(AROUND)):
        spec += in1[n].astype(F32)
    found = adjoint_modes(spec, target[...], None, resp_real, resp_imag, fields, tab)
    slope = core_gradient(found, tab, 0, TILE, 0, TILE)
    own_soft = soft[...]
    new = mask[...] - (STEP / (WIN * WIN)) * (slope * (0.25 - own_soft * own_soft))
    first[...] = new

    own_soft = above_half(new)
    soft[...] = own_soft
    parts = spectrum_parts(own_soft.astype(BF16), tab["col2"], tab["row2"], 2)
    for n, (di, dj) in enumerate(BACK):
        out2[n] = part_of(parts, di, dj).astype(out2.dtype)
    start(BACK, copies2)
    arrive(BACK, copies_goal)
    goal = jnp.concatenate(
        [
            jnp.concatenate([target[HALF:, HALF:], goals[2]], 1),
            jnp.concatenate([goals[1], goals[0]], 1),
        ],
        0,
    )
    row_at = lax.broadcasted_iota(jnp.int32, (TILE, TILE), 0)
    col_at = lax.broadcasted_iota(jnp.int32, (TILE, TILE), 1)
    row_end = jnp.where(row < n_row - 1, TILE, HALF)
    col_end = jnp.where(col < n_col - 1, TILE, HALF)
    counted = jnp.logical_and(row_at < row_end, col_at < col_end)
    arrive(BACK, copies2)
    spec = part_of(parts, 0, 0) + base2[...]
    for n in range(len(BACK)):
        spec += in2[n].astype(F32)
    found = adjoint_modes(spec, goal, counted, resp_real, resp_imag, fields, tab)
    out3[...] = found
    start(AHEAD, copies3)

    quarters = ((0, 0),) + AHEAD

    def save_quarter(n):
        di, dj = quarters[n]
        here = (pl.ds(0 if di else HALF, HALF), pl.ds(0 if dj else HALF, HALF))
        return pltpu.make_async_copy(moved.at[n], out.at[here], save.at[n])

    def finish(n, modes):
        di, dj = quarters[n]
        at_row, at_col = (0 if di else HALF), (0 if dj else HALF)
        slope = core_gradient(modes, tab, HALF - at_row, HALF, HALF - at_col, HALF)
        own_soft = soft[at_row : at_row + HALF, at_col : at_col + HALF]
        before = first[at_row : at_row + HALF, at_col : at_col + HALF]
        after = before - (STEP / (WIN * WIN)) * (slope * (0.25 - own_soft * own_soft))
        moved[n] = jnp.where(there(-di, -dj), after, before)
        save_quarter(n).start()

    finish(0, found)
    arrive(AHEAD, copies3)
    for n in range(len(AHEAD)):
        finish(n + 1, in3[n])

    sent(AROUND, copies1)
    sent(BACK, copies_goal)
    sent(BACK, copies2)
    sent(AHEAD, copies3)
    for n in range(len(quarters)):
        save_quarter(n).wait()


def solution(mesh):
    sizes = (mesh.shape["row"], mesh.shape["col"])
    made = tables()
    held = [made[name] for name in NAMES + ABSENT]

    def per_device(mask_param, target, kernel_modes, kernel_weight):
        message = (MODES, PAIR)
        return pl.pallas_call(
            functools.partial(kernel, sizes),
            out_shape=jax.ShapeDtypeStruct((TILE, TILE), F32),
            in_specs=[pl.BlockSpec(memory_space=pltpu.SMEM)]
            + [pl.BlockSpec(memory_space=pltpu.HBM)] * (3 + len(held)),
            out_specs=pl.BlockSpec(memory_space=pltpu.HBM),
            scratch_shapes=[
                pltpu.VMEM((TILE, TILE), F32),
                pltpu.VMEM((TILE, TILE), BF16),
                pltpu.VMEM((KERN,) + message, F32),
            ]
            + [pltpu.VMEM(made[name].shape, BF16) for name in NAMES]
            + [
                pltpu.VMEM((KERN,) + message, F32),
                pltpu.VMEM((KERN,) + message, F32),
                pltpu.VMEM((KERN, GRID, 2 * GRID), BF16),
                pltpu.VMEM((TILE, TILE), F32),
                pltpu.VMEM((TILE, TILE), F32),
                pltpu.VMEM((len(AROUND),) + message, BF16),
                pltpu.VMEM((len(AROUND),) + message, BF16),
                pltpu.VMEM((len(BACK),) + message, BF16),
                pltpu.VMEM((len(BACK),) + message, BF16),
                pltpu.VMEM(message, BF16),
                pltpu.VMEM((len(AHEAD),) + message, BF16),
                pltpu.VMEM((len(BACK), HALF, HALF), BF16),
                pltpu.VMEM(message, F32),
                pltpu.VMEM(message, F32),
            ]
            + [
                pltpu.SemaphoreType.DMA((count,))
                for count in (8, 8, 3, 3, 3, 3, 3, 3, 3 + len(NAMES), 2)
            ]
            + [pltpu.VMEM((4, HALF, HALF), F32), pltpu.SemaphoreType.DMA((4,))],
            compiler_params=pltpu.CompilerParams(
                collective_id=0, has_side_effects=True, vmem_limit_bytes=60 * 1024 * 1024
            ),
            cost_estimate=pl.CostEstimate(
                flops=1_000_000_000, bytes_accessed=3_000_000, transcendentals=300_000
            ),
        )(kernel_weight, mask_param, target, kernel_modes, *[jnp.asarray(t) for t in held])

    spread = P(("grp", "row"), "col")
    return jax.shard_map(
        per_device, mesh=mesh, in_specs=(spread, spread, P(), P()), out_specs=spread,
        check_vma=False,
    )
```

```python
import functools

import jax
import jax.numpy as jnp
import ml_dtypes
import numpy as np
from jax import lax
from jax.experimental import pallas as pl
from jax.experimental.pallas import tpu as pltpu
from jax.sharding import PartitionSpec as P

TILE = 256
MARGIN = 64
MODES = 64
KERN = 12
HALF = 128
WIN = 384
GRID = 128
PAIR = 2 * MODES
GROUP = 4

STEEPNESS = 4.0
THRESHOLD = 0.4
STEP = 16.0

MESH = pl.DeviceIdType.MESH
F32 = jnp.float32
BF16 = jnp.bfloat16

AROUND = ((1, 1), (1, -1), (-1, 1), (-1, -1), (1, 0), (-1, 0), (0, 1), (0, -1))
BACK = ((-1, -1), (-1, 0), (0, -1))
AHEAD = ((1, 1), (1, 0), (0, 1))
FIRST_AT = {-1: TILE + MARGIN, 0: MARGIN, 1: MARGIN - TILE}
SECOND_AT = {-1: TILE - MARGIN, 0: -MARGIN}


def cos_sin(places):
    places = np.asarray(places)
    frequency = np.arange(MODES) - MODES // 2
    angle = np.mod(frequency[:, None] * places[None, :], WIN) * (2.0 * np.pi / WIN)
    inside = ((places >= 0) & (places < WIN))[None, :]
    return np.where(inside, np.cos(angle), 0.0), np.where(inside, np.sin(angle), 0.0)


def tables():
    own = np.arange(TILE)

    def columns(offsets):
        parts = [cos_sin(own + offset) for offset in offsets]
        real = [np.concatenate([c.T, -s.T], 1) for c, s in parts]
        imag = [np.concatenate([s.T, c.T], 1) for c, s in parts]
        return np.concatenate(real + imag, 1)

    def rows(offsets):
        parts = [cos_sin(own + offset) for offset in offsets]
        return np.concatenate([np.concatenate([c, -s], 1) for c, s in parts], 0)

    first_at = [FIRST_AT[d] for d in (-1, 0, 1)]
    second_at = [SECOND_AT[d] for d in (-1, 0)]
    c3, s3 = cos_sin(np.arange(GRID) * (WIN // GRID))
    core_c, core_s = cos_sin(own + MARGIN)
    shift = (own + MARGIN)[:, None] / WIN - np.arange(GRID)[None, :] / GRID
    waves = np.arange(1, MODES)[:, None, None] * shift[None]
    resample = (1.0 + 2.0 * np.cos(2.0 * np.pi * waves).sum(0)) / GRID
    made = dict(
        col1=columns(first_at),
        row1=rows(first_at),
        col2=columns(second_at),
        row2=rows(second_at),
        inv3=np.block([[c3, s3], [-s3, c3]]),
        lift=np.concatenate([c3, s3], 0).T,
        up=resample,
        down=resample.T,
        adj=np.block([[c3.T, -s3.T, -s3.T, -c3.T], [s3.T, c3.T, c3.T, -s3.T]]),
        fold=np.concatenate([c3, s3], 1),
        invc=np.block([[core_c, core_s], [-core_s, core_c]]),
        rowc=np.concatenate([core_c.T, -core_s.T], 1),
    )
    held = {name: value.astype(ml_dtypes.bfloat16) for name, value in made.items()}

    def minus_half(di, dj, at):
        down_c, down_s = (t.sum(1, keepdims=True) for t in cos_sin(own + at[di]))
        over_c, over_s = (t.sum(1)[None] for t in cos_sin(own + at[dj]))
        real = down_c * over_c - down_s * over_s
        imag = -(down_c * over_s + down_s * over_c)
        return np.concatenate([real, imag], 1) * (-0.5 / (WIN * WIN))

    def empty(ways, at, states, missing):
        made = []
        for state in range(states):
            total = np.zeros((MODES, PAIR))
            for di, dj in ways:
                if missing(state, di, dj):
                    total += minus_half(di, dj, at)
            made.append(total)
        return np.stack(made).astype(np.float32)

    held["none1"] = empty(
        AROUND,
        FIRST_AT,
        16,
        lambda n, di, dj: (
            (di > 0 and n & 1) or (di < 0 and n & 2) or (dj > 0 and n & 4) or (dj < 0 and n & 8)
        ),
    )
    held["none2"] = empty(
        BACK, SECOND_AT, 4, lambda n, di, dj: (di < 0 and n & 1) or (dj < 0 and n & 2)
    )
    return held


NAMES = (
    "col1", "row1", "col2", "row2", "inv3", "lift",
    "up", "down", "adj", "fold", "invc", "rowc",
)
ABSENT = ("none1", "none2")


def dot(a, b):
    return jnp.dot(a, b, preferred_element_type=F32)


def above_half(x):
    return 0.5 * jnp.tanh(0.5 * x)


def low_half():
    return lax.broadcasted_iota(jnp.int32, (MODES, PAIR), 1) < MODES


def turned(pair):
    other = pltpu.roll(pair, MODES, 1)
    return jnp.where(low_half(), -other, other)


def spectrum_parts(wire, col, row, count):
    wide = PAIR * count
    half = dot(wire, col[...]).astype(BF16)
    stacked = jnp.concatenate([half[:, :wide], half[:, wide:]], 0)
    scale = 1.0 / (WIN * WIN)
    return [
        dot(row[n * MODES : (n + 1) * MODES], stacked) * scale for n in range(count)
    ]


def adjoint_modes(spec, goal, counted, resp_real, resp_imag, fields, tab):
    other = turned(spec)
    lifted = []
    for k in range(0, KERN, 2):
        pair = []
        for n in (k, k + 1):
            filtered = resp_real[n] * spec + resp_imag[n] * other
            rotated = resp_real[n] * other - resp_imag[n] * spec
            pair.append(jnp.concatenate([filtered.astype(BF16), rotated.astype(BF16)], 0))
        both = dot(tab["lift"][...], jnp.concatenate(pair, 1)).astype(BF16)
        lifted += [both[:, :PAIR], both[:, PAIR:]]
    level = jnp.zeros((GRID, GRID), F32)
    for k in range(0, KERN, GROUP):
        group = dot(jnp.concatenate(lifted[k : k + GROUP], 0), tab["inv3"][...])
        for n in range(GROUP):
            field = group[n * GRID : (n + 1) * GRID]
            fields[k + n] = field.astype(BF16)
            level += field[:, :GRID] * field[:, :GRID] + field[:, GRID:] * field[:, GRID:]
    across = dot(level.astype(BF16), tab["down"][...]).astype(BF16)
    core = dot(tab["up"][...], across)
    printed = above_half(STEEPNESS * (core - THRESHOLD))
    pull = (4.0 * STEEPNESS) * (printed + (0.5 - goal.astype(F32))) * (0.25 - printed * printed)
    if counted is not None:
        pull = jnp.where(counted, pull, 0.0)
    pull = dot(pull.astype(BF16), tab["up"][...]).astype(BF16)
    pull = dot(tab["down"][...], pull)
    pull = pull.astype(BF16)
    both = jnp.concatenate([pull, pull], 1)
    sum_real = jnp.zeros((MODES, PAIR), F32)
    sum_imag = jnp.zeros((MODES, PAIR), F32)
    for k in range(0, KERN, 2):
        scaled = jnp.concatenate([fields[k] * both, fields[k + 1] * both], 0)
        back = dot(scaled, tab["adj"][...]).astype(BF16)
        one, two = back[:GRID], back[GRID:]
        upper = jnp.concatenate([one[:, :PAIR], two[:, :PAIR]], 1)
        lower = jnp.concatenate([one[:, PAIR:], two[:, PAIR:]], 1)
        modes = dot(tab["fold"][...], jnp.concatenate([upper, lower], 0))
        for n in range(2):
            half = modes[:, n * PAIR : (n + 1) * PAIR]
            sum_real += resp_real[k + n] * half
            sum_imag += resp_imag[k + n] * half
    return (sum_real - turned(sum_imag)).astype(BF16)


def core_gradient(modes, tab, low_row, rows, low_col, cols):
    part = jnp.concatenate(
        [
            tab["invc"][:, low_col : low_col + cols],
            tab["invc"][:, TILE + low_col : TILE + low_col + cols],
        ],
        1,
    )
    partial = dot(modes, part).astype(BF16)
    stacked = jnp.concatenate([partial[:, :cols], partial[:, cols:]], 0)
    return dot(tab["rowc"][low_row : low_row + rows], stacked)


def kernel(sizes, weight, *refs):
    count = 3 + len(NAMES)
    far, (none1, none2), refs = refs[:count], refs[count : count + 2], refs[count + 2 :]
    out, near, refs = refs[0], refs[1 : 1 + count], refs[1 + count :]
    mask, target, modes = near[:3]
    tab = dict(zip(NAMES, near[3:]))
    (
        resp_real, resp_imag, fields, first, soft,
        out1, in1, out2, in2, out3, in3, goals, base1, base2,
        send1, recv1, send2, recv2, send3, recv3, send_goal, recv_goal, load, none_sem,
        moved, save,
    ) = refs
    n_row, n_col = sizes
    row, col = lax.axis_index("row"), lax.axis_index("col")

    def there(di, dj):
        ok_row = {-1: row >= 1, 0: row >= 0, 1: row < n_row - 1}[di]
        ok_col = {-1: col >= 1, 0: col >= 0, 1: col < n_col - 1}[dj]
        return jnp.logical_and(ok_row, ok_col)

    def place(di, dj):
        return {"row": row + di, "col": col + dj}

    barrier = pltpu.get_barrier_semaphore()
    for di, dj in AROUND:

        @pl.when(there(di, dj))
        def _():
            pl.semaphore_signal(barrier, inc=1, device_id=place(di, dj), device_id_type=MESH)

    order = ("mask", "col1", "row1", "target", "modes") + NAMES[2:]
    slot = {"mask": 0, "target": 1, "modes": 2} | {n: 3 + k for k, n in enumerate(NAMES)}
    loads = {
        name: pltpu.make_async_copy(far[slot[name]], near[slot[name]], load.at[slot[name]])
        for name in order
    }
    for name in order[:3]:
        loads[name].start()
    edges = [(row == 0), (row == n_row - 1), (col == 0), (col == n_col - 1)]
    up, down, left, right = [edge.astype(jnp.int32) for edge in edges]
    load_none1 = pltpu.make_async_copy(
        none1.at[up + 2 * down + 4 * left + 8 * right], base1, none_sem.at[0]
    )
    load_none2 = pltpu.make_async_copy(none2.at[down + 2 * right], base2, none_sem.at[1])
    load_none1.start()
    load_none2.start()
    for name in order[3:]:
        loads[name].start()

    def copies(ways, source, landing, send, recv):
        return [
            pltpu.make_async_remote_copy(
                src_ref=source(n),
                dst_ref=landing.at[n],
                send_sem=send.at[n],
                recv_sem=recv.at[n],
                device_id=place(di, dj),
                device_id_type=MESH,
            )
            for n, (di, dj) in enumerate(ways)
        ]

    def start(ways, group):
        for (di, dj), copy in zip(ways, group):

            @pl.when(there(di, dj))
            def _():
                copy.start()

    def arrive(ways, group):
        for (di, dj), copy in zip(ways, group):

            @pl.when(there(-di, -dj))
            def _():
                copy.wait_recv()

    def sent(ways, group):
        for (di, dj), copy in zip(ways, group):

            @pl.when(there(di, dj))
            def _():
                copy.wait_send()

    def blank(ways, landing):
        for n, (di, dj) in enumerate(ways):

            @pl.when(jnp.logical_not(there(-di, -dj)))
            def _():
                landing[n] = jnp.zeros(landing.shape[1:], landing.dtype)

    corner = {-1: 0, 0: HALF}
    copies1 = copies(AROUND, lambda n: out1.at[n], in1, send1, recv1)
    copies2 = copies(BACK, lambda n: out2.at[n], in2, send2, recv2)
    copies3 = copies(AHEAD, lambda n: out3, in3, send3, recv3)
    copies_goal = copies(
        BACK,
        lambda n: target.at[
            pl.ds(corner[BACK[n][0]], HALF), pl.ds(corner[BACK[n][1]], HALF)
        ],
        goals,
        send_goal,
        recv_goal,
    )

    for name in ("mask", "col1", "row1"):
        loads[name].wait()
    own_soft = above_half(mask[...])
    soft[...] = own_soft
    parts = spectrum_parts(own_soft.astype(BF16), tab["col1"], tab["row1"], 3)

    def part_of(parts, di, dj):
        return parts[di + 1][:, (dj + 1) * PAIR : (dj + 2) * PAIR]

    for n, (di, dj) in enumerate(AROUND):
        out1[n] = part_of(parts, di, dj).astype(out1.dtype)
    rows_around = 1 + (row >= 1).astype(jnp.int32) + (row < n_row - 1).astype(jnp.int32)
    cols_around = 1 + (col >= 1).astype(jnp.int32) + (col < n_col - 1).astype(jnp.int32)
    pl.semaphore_wait(barrier, rows_around * cols_around - 1)
    start(AROUND, copies1)

    blank(AROUND, in1)
    blank(BACK, in2)
    blank(AHEAD, in3)
    blank(BACK, goals)
    loads["modes"].wait()
    for k in range(KERN):
        pair = modes[k] * jnp.sqrt(jnp.full((MODES, PAIR), weight[k], F32))
        other = pltpu.roll(pair, MODES, 1)
        resp_real[k] = jnp.where(low_half(), pair, other)
        resp_imag[k] = jnp.where(low_half(), other, pair)

    for name in ("target",) + NAMES[2:]:
        loads[name].wait()
    load_none1.wait()
    load_none2.wait()
    arrive(AROUND, copies1)
    start(BACK, copies_goal)
    spec = part_of(parts, 0, 0) + base1[...]
    for n in range(len(AROUND)):
        spec += in1[n].astype(F32)
    found = adjoint_modes(spec, target[...], None, resp_real, resp_imag, fields, tab)
    slope = core_gradient(found, tab, 0, TILE, 0, TILE)
    own_soft = soft[...]
    new = mask[...] - (STEP / (WIN * WIN)) * (slope * (0.25 - own_soft * own_soft))
    first[...] = new

    own_soft = above_half(new)
    soft[...] = own_soft
    parts = spectrum_parts(own_soft.astype(BF16), tab["col2"], tab["row2"], 2)
    for n, (di, dj) in enumerate(BACK):
        out2[n] = part_of(parts, di, dj).astype(out2.dtype)
    start(BACK, copies2)
    arrive(BACK, copies_goal)
    goal = jnp.concatenate(
        [
            jnp.concatenate([target[HALF:, HALF:], goals[2]], 1),
            jnp.concatenate([goals[1], goals[0]], 1),
        ],
        0,
    )
    row_at = lax.broadcasted_iota(jnp.int32, (TILE, TILE), 0)
    col_at = lax.broadcasted_iota(jnp.int32, (TILE, TILE), 1)
    row_end = jnp.where(row < n_row - 1, TILE, HALF)
    col_end = jnp.where(col < n_col - 1, TILE, HALF)
    counted = jnp.logical_and(row_at < row_end, col_at < col_end)
    arrive(BACK, copies2)
    spec = part_of(parts, 0, 0) + base2[...]
    for n in range(len(BACK)):
        spec += in2[n].astype(F32)
    found = adjoint_modes(spec, goal, counted, resp_real, resp_imag, fields, tab)
    out3[...] = found
    start(AHEAD, copies3)

    quarters = ((0, 0),) + AHEAD

    def save_quarter(n):
        di, dj = quarters[n]
        here = (pl.ds(0 if di else HALF, HALF), pl.ds(0 if dj else HALF, HALF))
        return pltpu.make_async_copy(moved.at[n], out.at[here], save.at[n])

    def finish(n, modes):
        di, dj = quarters[n]
        at_row, at_col = (0 if di else HALF), (0 if dj else HALF)
        slope = core_gradient(modes, tab, HALF - at_row, HALF, HALF - at_col, HALF)
        own_soft = soft[at_row : at_row + HALF, at_col : at_col + HALF]
        before = first[at_row : at_row + HALF, at_col : at_col + HALF]
        after = before - (STEP / (WIN * WIN)) * (slope * (0.25 - own_soft * own_soft))
        moved[n] = jnp.where(there(-di, -dj), after, before)
        save_quarter(n).start()

    finish(0, found)
    arrive(AHEAD, copies3)
    for n in range(len(AHEAD)):
        finish(n + 1, in3[n])

    sent(AROUND, copies1)
    sent(BACK, copies_goal)
    sent(BACK, copies2)
    sent(AHEAD, copies3)
    for n in range(len(quarters)):
        save_quarter(n).wait()


def solution(mesh):
    sizes = (mesh.shape["row"], mesh.shape["col"])
    made = tables()
    held = [made[name] for name in NAMES + ABSENT]

    def per_device(mask_param, target, kernel_modes, kernel_weight):
        message = (MODES, PAIR)
        return pl.pallas_call(
            functools.partial(kernel, sizes),
            out_shape=jax.ShapeDtypeStruct((TILE, TILE), F32),
            in_specs=[pl.BlockSpec(memory_space=pltpu.SMEM)]
            + [pl.BlockSpec(memory_space=pltpu.HBM)] * (3 + len(held)),
            out_specs=pl.BlockSpec(memory_space=pltpu.HBM),
            scratch_shapes=[
                pltpu.VMEM((TILE, TILE), F32),
                pltpu.VMEM((TILE, TILE), BF16),
                pltpu.VMEM((KERN,) + message, F32),
            ]
            + [pltpu.VMEM(made[name].shape, BF16) for name in NAMES]
            + [
                pltpu.VMEM((KERN,) + message, F32),
                pltpu.VMEM((KERN,) + message, F32),
                pltpu.VMEM((KERN, GRID, 2 * GRID), BF16),
                pltpu.VMEM((TILE, TILE), F32),
                pltpu.VMEM((TILE, TILE), F32),
                pltpu.VMEM((len(AROUND),) + message, BF16),
                pltpu.VMEM((len(AROUND),) + message, BF16),
                pltpu.VMEM((len(BACK),) + message, BF16),
                pltpu.VMEM((len(BACK),) + message, BF16),
                pltpu.VMEM(message, BF16),
                pltpu.VMEM((len(AHEAD),) + message, BF16),
                pltpu.VMEM((len(BACK), HALF, HALF), BF16),
                pltpu.VMEM(message, F32),
                pltpu.VMEM(message, F32),
            ]
            + [
                pltpu.SemaphoreType.DMA((count,))
                for count in (8, 8, 3, 3, 3, 3, 3, 3, 3 + len(NAMES), 2)
            ]
            + [pltpu.VMEM((4, HALF, HALF), F32), pltpu.SemaphoreType.DMA((4,))],
            compiler_params=pltpu.CompilerParams(
                collective_id=0, has_side_effects=True, vmem_limit_bytes=60 * 1024 * 1024
            ),
            cost_estimate=pl.CostEstimate(
                flops=1_000_000_000, bytes_accessed=3_000_000, transcendentals=300_000
            ),
        )(kernel_weight, mask_param, target, kernel_modes, *[jnp.asarray(t) for t in held])

    spread = P(("grp", "row"), "col")
    return jax.shard_map(
        per_device, mesh=mesh, in_specs=(spread, spread, P(), P()), out_specs=spread,
        check_vma=False,
    )
```

```python
import functools

import jax
import jax.numpy as jnp
import ml_dtypes
import numpy as np
from jax import lax
from jax.experimental import pallas as pl
from jax.experimental.pallas import tpu as pltpu
from jax.sharding import PartitionSpec as P

TILE = 256
MARGIN = 64
MODES = 64
KERN = 12
HALF = 128
WIN = 384
GRID = 128
PAIR = 2 * MODES

STEEPNESS = 4.0
THRESHOLD = 0.4
STEP = 16.0

MESH = pl.DeviceIdType.MESH
F32 = jnp.float32
BF16 = jnp.bfloat16

AROUND = ((1, 1), (1, -1), (-1, 1), (-1, -1), (1, 0), (-1, 0), (0, 1), (0, -1))
BACK = ((-1, -1), (-1, 0), (0, -1))
AHEAD = ((1, 1), (1, 0), (0, 1))
FIRST_AT = {-1: TILE + MARGIN, 0: MARGIN, 1: MARGIN - TILE}
SECOND_AT = {-1: TILE - MARGIN, 0: -MARGIN}


def cos_sin(places):
    places = np.asarray(places)
    frequency = np.arange(MODES) - MODES // 2
    angle = np.mod(frequency[:, None] * places[None, :], WIN) * (2.0 * np.pi / WIN)
    inside = ((places >= 0) & (places < WIN))[None, :]
    return np.where(inside, np.cos(angle), 0.0), np.where(inside, np.sin(angle), 0.0)


def tables():
    own = np.arange(TILE)

    def columns(offsets):
        parts = [cos_sin(own + offset) for offset in offsets]
        real = [np.concatenate([c.T, -s.T], 1) for c, s in parts]
        imag = [np.concatenate([s.T, c.T], 1) for c, s in parts]
        return np.concatenate(real + imag, 1)

    def rows(offsets):
        parts = [cos_sin(own + offset) for offset in offsets]
        return np.concatenate([np.concatenate([c, -s], 1) for c, s in parts], 0)

    first_at = [FIRST_AT[d] for d in (-1, 0, 1)]
    second_at = [SECOND_AT[d] for d in (-1, 0)]
    c3, s3 = cos_sin(np.arange(GRID) * (WIN // GRID))
    core_c, core_s = cos_sin(own + MARGIN)
    shift = (own + MARGIN)[:, None] / WIN - np.arange(GRID)[None, :] / GRID
    waves = np.arange(1, MODES)[:, None, None] * shift[None]
    resample = (1.0 + 2.0 * np.cos(2.0 * np.pi * waves).sum(0)) / GRID
    made = dict(
        col1=columns(first_at),
        row1=rows(first_at),
        col2=columns(second_at),
        row2=rows(second_at),
        inv3=np.block([[c3, s3], [-s3, c3]]),
        lift=np.concatenate([c3, s3], 0).T,
        up=resample,
        down=resample.T,
        adj=np.block([[c3.T, -s3.T, -s3.T, -c3.T], [s3.T, c3.T, c3.T, -s3.T]]),
        fold=np.concatenate([c3, s3], 1),
        invc=np.block([[core_c, core_s], [-core_s, core_c]]),
        rowc=np.concatenate([core_c.T, -core_s.T], 1),
    )
    held = {name: value.astype(ml_dtypes.bfloat16) for name, value in made.items()}

    def minus_half(di, dj, at):
        down_c, down_s = (t.sum(1, keepdims=True) for t in cos_sin(own + at[di]))
        over_c, over_s = (t.sum(1)[None] for t in cos_sin(own + at[dj]))
        real = down_c * over_c - down_s * over_s
        imag = -(down_c * over_s + down_s * over_c)
        return np.concatenate([real, imag], 1) * (-0.5 / (WIN * WIN))

    def empty(ways, at, states, missing):
        made = []
        for state in range(states):
            total = np.zeros((MODES, PAIR))
            for di, dj in ways:
                if missing(state, di, dj):
                    total += minus_half(di, dj, at)
            made.append(total)
        return np.stack(made).astype(np.float32)

    held["none1"] = empty(
        AROUND,
        FIRST_AT,
        16,
        lambda n, di, dj: (
            (di > 0 and n & 1) or (di < 0 and n & 2) or (dj > 0 and n & 4) or (dj < 0 and n & 8)
        ),
    )
    held["none2"] = empty(
        BACK, SECOND_AT, 4, lambda n, di, dj: (di < 0 and n & 1) or (dj < 0 and n & 2)
    )
    return held


NAMES = (
    "col1", "row1", "col2", "row2", "inv3", "lift",
    "up", "down", "adj", "fold", "invc", "rowc",
)
ABSENT = ("none1", "none2")


def dot(a, b):
    return jnp.dot(a, b, preferred_element_type=F32)


def above_half(x):
    return 0.5 * jnp.tanh(0.5 * x)


def low_half():
    return lax.broadcasted_iota(jnp.int32, (MODES, PAIR), 1) < MODES


def turned(pair):
    other = pltpu.roll(pair, MODES, 1)
    return jnp.where(low_half(), -other, other)


def spectrum_parts(wire, col, row, count):
    wide = PAIR * count
    half = dot(wire, col[...]).astype(BF16)
    stacked = jnp.concatenate([half[:, :wide], half[:, wide:]], 0)
    return dot(row[...], stacked) * (1.0 / (WIN * WIN))


def adjoint_modes(spec, goal, counted, resp_real, resp_imag, fields, tab):
    other = turned(spec)
    pairs = []
    for k in range(KERN):
        filtered = resp_real[k] * spec + resp_imag[k] * other
        rotated = resp_real[k] * other - resp_imag[k] * spec
        pairs.append(jnp.concatenate([filtered.astype(BF16), rotated.astype(BF16)], 0))
    lifted = dot(tab["lift"][...], jnp.concatenate(pairs, 1)).astype(BF16)
    lifted = [lifted[:, k * PAIR : (k + 1) * PAIR] for k in range(KERN)]
    field = dot(jnp.concatenate(lifted, 0), tab["inv3"][...]).reshape(KERN, GRID, 2 * GRID)
    fields[...] = field.astype(BF16)
    power = jnp.sum(field * field, 0)
    level = power[:, :GRID] + power[:, GRID:]
    across = dot(level.astype(BF16), tab["down"][...]).astype(BF16)
    core = dot(tab["up"][...], across)
    printed = above_half(STEEPNESS * (core - THRESHOLD))
    pull = (4.0 * STEEPNESS) * (printed + (0.5 - goal.astype(F32))) * (0.25 - printed * printed)
    if counted is not None:
        pull = jnp.where(counted, pull, 0.0)
    pull = dot(pull.astype(BF16), tab["up"][...]).astype(BF16)
    pull = dot(tab["down"][...], pull)
    pull = pull.astype(BF16)
    both = jnp.concatenate([pull, pull], 1)
    scaled = (fields[...] * both[None]).reshape(KERN * GRID, 2 * GRID)
    back = dot(scaled, tab["adj"][...]).astype(BF16)
    sum_real = jnp.zeros((MODES, PAIR), F32)
    sum_imag = jnp.zeros((MODES, PAIR), F32)
    stacked = []
    for k in range(KERN):
        one = back[k * GRID : (k + 1) * GRID]
        stacked.append(jnp.concatenate([one[:, :PAIR], one[:, PAIR:]], 0))
    modes = dot(tab["fold"][...], jnp.concatenate(stacked, 1))
    for k in range(KERN):
        one = modes[:, k * PAIR : (k + 1) * PAIR]
        sum_real += resp_real[k] * one
        sum_imag += resp_imag[k] * one
    return (sum_real - turned(sum_imag)).astype(BF16)


def core_gradient(modes, tab, low_row, rows, low_col, cols):
    part = jnp.concatenate(
        [
            tab["invc"][:, low_col : low_col + cols],
            tab["invc"][:, TILE + low_col : TILE + low_col + cols],
        ],
        1,
    )
    partial = dot(modes, part).astype(BF16)
    stacked = jnp.concatenate([partial[:, :cols], partial[:, cols:]], 0)
    return dot(tab["rowc"][low_row : low_row + rows], stacked)


def kernel(sizes, weight, *refs):
    count = 3 + len(NAMES)
    far, (none1, none2), refs = refs[:count], refs[count : count + 2], refs[count + 2 :]
    out, near, refs = refs[0], refs[1 : 1 + count], refs[1 + count :]
    mask, target, modes = near[:3]
    tab = dict(zip(NAMES, near[3:]))
    (
        resp_real, resp_imag, fields, first, soft,
        out1, in1, out2, in2, out3, in3, goals, base1, base2,
        send1, recv1, send2, recv2, send3, recv3, send_goal, recv_goal, load, none_sem,
        moved, save,
    ) = refs
    n_row, n_col = sizes
    row, col = lax.axis_index("row"), lax.axis_index("col")

    def there(di, dj):
        ok_row = {-1: row >= 1, 0: row >= 0, 1: row < n_row - 1}[di]
        ok_col = {-1: col >= 1, 0: col >= 0, 1: col < n_col - 1}[dj]
        return jnp.logical_and(ok_row, ok_col)

    def place(di, dj):
        return {"row": row + di, "col": col + dj}

    barrier = pltpu.get_barrier_semaphore()
    for di, dj in AROUND:

        @pl.when(there(di, dj))
        def _():
            pl.semaphore_signal(barrier, inc=1, device_id=place(di, dj), device_id_type=MESH)

    order = ("mask", "col1", "row1", "target", "modes") + NAMES[2:]
    slot = {"mask": 0, "target": 1, "modes": 2} | {n: 3 + k for k, n in enumerate(NAMES)}
    loads = {
        name: pltpu.make_async_copy(far[slot[name]], near[slot[name]], load.at[slot[name]])
        for name in order
    }
    for name in order:
        loads[name].start()
    edges = [(row == 0), (row == n_row - 1), (col == 0), (col == n_col - 1)]
    up, down, left, right = [edge.astype(jnp.int32) for edge in edges]
    load_none1 = pltpu.make_async_copy(
        none1.at[up + 2 * down + 4 * left + 8 * right], base1, none_sem.at[0]
    )
    load_none2 = pltpu.make_async_copy(none2.at[down + 2 * right], base2, none_sem.at[1])
    load_none1.start()
    load_none2.start()

    def copies(ways, source, landing, send, recv):
        return [
            pltpu.make_async_remote_copy(
                src_ref=source(n),
                dst_ref=landing.at[n],
                send_sem=send.at[n],
                recv_sem=recv.at[n],
                device_id=place(di, dj),
                device_id_type=MESH,
            )
            for n, (di, dj) in enumerate(ways)
        ]

    def start(ways, group):
        for (di, dj), copy in zip(ways, group):

            @pl.when(there(di, dj))
            def _():
                copy.start()

    def arrive(ways, group):
        for (di, dj), copy in zip(ways, group):

            @pl.when(there(-di, -dj))
            def _():
                copy.wait_recv()

    def sent(ways, group):
        for (di, dj), copy in zip(ways, group):

            @pl.when(there(di, dj))
            def _():
                copy.wait_send()

    def blank(ways, landing):
        for n, (di, dj) in enumerate(ways):

            @pl.when(jnp.logical_not(there(-di, -dj)))
            def _():
                landing[n] = jnp.zeros(landing.shape[1:], landing.dtype)

    corner = {-1: 0, 0: HALF}
    copies1 = copies(AROUND, lambda n: out1.at[n], in1, send1, recv1)
    copies2 = copies(BACK, lambda n: out2.at[n], in2, send2, recv2)
    copies3 = copies(AHEAD, lambda n: out3, in3, send3, recv3)
    copies_goal = copies(
        BACK,
        lambda n: target.at[
            pl.ds(corner[BACK[n][0]], HALF), pl.ds(corner[BACK[n][1]], HALF)
        ],
        goals,
        send_goal,
        recv_goal,
    )

    for name in ("mask", "col1", "row1"):
        loads[name].wait()
    own_soft = above_half(mask[...])
    soft[...] = own_soft
    parts = spectrum_parts(own_soft.astype(BF16), tab["col1"], tab["row1"], 3)

    def part_of(parts, di, dj):
        return parts[(di + 1) * MODES : (di + 2) * MODES, (dj + 1) * PAIR : (dj + 2) * PAIR]

    for n, (di, dj) in enumerate(AROUND):
        out1[n] = part_of(parts, di, dj).astype(out1.dtype)
    rows_around = 1 + (row >= 1).astype(jnp.int32) + (row < n_row - 1).astype(jnp.int32)
    cols_around = 1 + (col >= 1).astype(jnp.int32) + (col < n_col - 1).astype(jnp.int32)
    pl.semaphore_wait(barrier, rows_around * cols_around - 1)
    start(AROUND, copies1)

    blank(AROUND, in1)
    blank(BACK, in2)
    blank(AHEAD, in3)
    blank(BACK, goals)
    loads["modes"].wait()
    for k in range(KERN):
        pair = modes[k] * jnp.sqrt(jnp.full((MODES, PAIR), weight[k], F32))
        other = pltpu.roll(pair, MODES, 1)
        resp_real[k] = jnp.where(low_half(), pair, other)
        resp_imag[k] = jnp.where(low_half(), other, pair)

    for name in ("target",) + NAMES[2:]:
        loads[name].wait()
    load_none1.wait()
    load_none2.wait()
    arrive(AROUND, copies1)
    start(BACK, copies_goal)
    spec = part_of(parts, 0, 0) + base1[...]
    for n in range(len(AROUND)):
        spec += in1[n].astype(F32)
    found = adjoint_modes(spec, target[...], None, resp_real, resp_imag, fields, tab)
    slope = core_gradient(found, tab, 0, TILE, 0, TILE)
    own_soft = soft[...]
    new = mask[...] - (STEP / (WIN * WIN)) * (slope * (0.25 - own_soft * own_soft))
    first[...] = new

    own_soft = above_half(new)
    soft[...] = own_soft
    parts = spectrum_parts(own_soft.astype(BF16), tab["col2"], tab["row2"], 2)
    for n, (di, dj) in enumerate(BACK):
        out2[n] = part_of(parts, di, dj).astype(out2.dtype)
    start(BACK, copies2)
    arrive(BACK, copies_goal)
    goal = jnp.concatenate(
        [
            jnp.concatenate([target[HALF:, HALF:], goals[2]], 1),
            jnp.concatenate([goals[1], goals[0]], 1),
        ],
        0,
    )
    row_at = lax.broadcasted_iota(jnp.int32, (TILE, TILE), 0)
    col_at = lax.broadcasted_iota(jnp.int32, (TILE, TILE), 1)
    row_end = jnp.where(row < n_row - 1, TILE, HALF)
    col_end = jnp.where(col < n_col - 1, TILE, HALF)
    counted = jnp.logical_and(row_at < row_end, col_at < col_end)
    arrive(BACK, copies2)
    spec = part_of(parts, 0, 0) + base2[...]
    for n in range(len(BACK)):
        spec += in2[n].astype(F32)
    found = adjoint_modes(spec, goal, counted, resp_real, resp_imag, fields, tab)
    out3[...] = found
    start(AHEAD, copies3)

    quarters = ((0, 0),) + AHEAD

    def save_quarter(n):
        di, dj = quarters[n]
        here = (pl.ds(0 if di else HALF, HALF), pl.ds(0 if dj else HALF, HALF))
        return pltpu.make_async_copy(moved.at[n], out.at[here], save.at[n])

    def finish(n, modes):
        di, dj = quarters[n]
        at_row, at_col = (0 if di else HALF), (0 if dj else HALF)
        slope = core_gradient(modes, tab, HALF - at_row, HALF, HALF - at_col, HALF)
        own_soft = soft[at_row : at_row + HALF, at_col : at_col + HALF]
        before = first[at_row : at_row + HALF, at_col : at_col + HALF]
        after = before - (STEP / (WIN * WIN)) * (slope * (0.25 - own_soft * own_soft))
        moved[n] = jnp.where(there(-di, -dj), after, before)
        save_quarter(n).start()

    finish(0, found)
    arrive(AHEAD, copies3)
    for n in range(len(AHEAD)):
        finish(n + 1, in3[n])

    sent(AROUND, copies1)
    sent(BACK, copies_goal)
    sent(BACK, copies2)
    sent(AHEAD, copies3)
    for n in range(len(quarters)):
        save_quarter(n).wait()


def solution(mesh):
    sizes = (mesh.shape["row"], mesh.shape["col"])
    made = tables()
    held = [made[name] for name in NAMES + ABSENT]

    def per_device(mask_param, target, kernel_modes, kernel_weight):
        message = (MODES, PAIR)
        return pl.pallas_call(
            functools.partial(kernel, sizes),
            out_shape=jax.ShapeDtypeStruct((TILE, TILE), F32),
            in_specs=[pl.BlockSpec(memory_space=pltpu.SMEM)]
            + [pl.BlockSpec(memory_space=pltpu.HBM)] * (3 + len(held)),
            out_specs=pl.BlockSpec(memory_space=pltpu.HBM),
            scratch_shapes=[
                pltpu.VMEM((TILE, TILE), F32),
                pltpu.VMEM((TILE, TILE), BF16),
                pltpu.VMEM((KERN,) + message, F32),
            ]
            + [pltpu.VMEM(made[name].shape, BF16) for name in NAMES]
            + [
                pltpu.VMEM((KERN,) + message, F32),
                pltpu.VMEM((KERN,) + message, F32),
                pltpu.VMEM((KERN, GRID, 2 * GRID), BF16),
                pltpu.VMEM((TILE, TILE), F32),
                pltpu.VMEM((TILE, TILE), F32),
                pltpu.VMEM((len(AROUND),) + message, BF16),
                pltpu.VMEM((len(AROUND),) + message, BF16),
                pltpu.VMEM((len(BACK),) + message, BF16),
                pltpu.VMEM((len(BACK),) + message, BF16),
                pltpu.VMEM(message, BF16),
                pltpu.VMEM((len(AHEAD),) + message, BF16),
                pltpu.VMEM((len(BACK), HALF, HALF), BF16),
                pltpu.VMEM(message, F32),
                pltpu.VMEM(message, F32),
            ]
            + [
                pltpu.SemaphoreType.DMA((count,))
                for count in (8, 8, 3, 3, 3, 3, 3, 3, 3 + len(NAMES), 2)
            ]
            + [pltpu.VMEM((4, HALF, HALF), F32), pltpu.SemaphoreType.DMA((4,))],
            compiler_params=pltpu.CompilerParams(
                collective_id=0, has_side_effects=True, vmem_limit_bytes=60 * 1024 * 1024
            ),
            cost_estimate=pl.CostEstimate(
                flops=1_000_000_000, bytes_accessed=3_000_000, transcendentals=300_000
            ),
        )(kernel_weight, mask_param, target, kernel_modes, *[jnp.asarray(t) for t in held])

    spread = P(("grp", "row"), "col")
    return jax.shard_map(
        per_device, mesh=mesh, in_specs=(spread, spread, P(), P()), out_specs=spread,
        check_vma=False,
    )
```
